256 devices in a mesh: seq: 2 (over core), dp: 8 (over z), island: 16 (over y, x).
Axes of the slice: x: 4, y: 4, z: 8, core: 2. Of those that a mesh axis runs over, the one named last changes fastest.
Arguments:
- layer_input: bfloat16 [16, 8, 256, 8192], P('island', 'dp', 'seq'), may hold values from -6 to 6
- inner_acts: bfloat16 [16, 8, 256, 8192], P('island', 'dp', 'seq'), may hold values from -6 to 6
- out_grad: bfloat16 [16, 8, 256, 8192], P('island', 'dp', 'seq'), may hold values from -6 to 6
- step_sizes: float32 [16, 8, 256, 128], P('island', 'dp', 'seq'), may hold values from 0 to 1.2
- outer_weight: float32 [8192, 256], P(('seq', 'dp')), may hold values from -6 to 6
- island_drift: float32 [16, 8192, 256], P('island', ('seq', 'dp')), may hold values from -6 to 6
- momentum: float32 [8192, 256], P(('seq', 'dp')), may hold values from -6 to 6
Outputs:
- in_grad: bfloat16 [16, 8, 256, 8192], P('island', 'dp', 'seq')
- sel_grad: bfloat16 [16, 8, 256, 256], P('island', 'dp', 'seq')
- new_momentum: float32 [8192, 256], P(('seq', 'dp'))
- new_outer: float32 [8192, 256], P(('seq', 'dp'))
The draws below stay inside these ranges and needn't reach their ends.
All inputs are finite; a program needn't handle non-finite values.
Results may differ from the reference program's by a relative error of at most 0.007.
Values may be sent and summed in bfloat16 or wider, within the bound.
A program may use at most 192 MiB of HBM per device.

```python
import math
import jax
import jax.numpy as jnp
from jax import lax

D = 8192
LOCAL_HEADS = 128
HEAD_DIM = 64
STATE = 128
T_DEV = 128
HP = 8192
SEQUENCE_LENGTH = 256
N_DP = 8
N_ISLAND = 16


def draw_step_sizes(key, part):
    key = jax.random.fold_in(key, 7)
    random_subkeys = jax.random.split(key, 7)
    sequence_batch = N_ISLAND * N_DP
    slow_share = 5
    slow_heads = jax.random.randint(random_subkeys[0], (sequence_batch, 1, LOCAL_HEADS), 0, 10) < slow_share
    slow_rate = jnp.exp(jax.random.uniform(random_subkeys[1], (sequence_batch, 1, LOCAL_HEADS), jnp.float32, math.log(0.05), math.log(0.3))) * (math.log(10.0) / SEQUENCE_LENGTH)
    fast_rate = jnp.exp(jax.random.uniform(random_subkeys[2], (sequence_batch, 1, LOCAL_HEADS), jnp.float32, math.log(1.0 / 50.0), math.log(1.0 / 30.0)))
    baseline_rate = jnp.where(slow_heads, slow_rate, fast_rate)
    jitter_level = jax.random.uniform(random_subkeys[3], (sequence_batch, SEQUENCE_LENGTH, LOCAL_HEADS), jnp.float32, 0.5, 1.5)
    blocks = SEQUENCE_LENGTH // T_DEV
    worker_multiplier = jnp.exp(jax.random.uniform(random_subkeys[4], (sequence_batch, blocks, 1, 1), jnp.float32, -0.35, 0.35))
    worker_multiplier = jnp.broadcast_to(worker_multiplier, (sequence_batch, blocks, T_DEV, 1)).reshape(sequence_batch, SEQUENCE_LENGTH, 1)
    spike_position = jax.random.randint(random_subkeys[5], (sequence_batch, 2, 1), 0, SEQUENCE_LENGTH)
    token_positions = jnp.arange(SEQUENCE_LENGTH)
    spike_flags = jnp.sum((token_positions[None, None, :] == spike_position).astype(jnp.float32), axis=1)
    spike_magnitude = jax.random.uniform(random_subkeys[6], (sequence_batch, 1, LOCAL_HEADS), jnp.float32, 0.2, 0.5)
    step_amounts = baseline_rate * jitter_level * worker_multiplier + spike_flags[:, :, None] * spike_magnitude
    return step_amounts.reshape(N_ISLAND, N_DP, SEQUENCE_LENGTH, LOCAL_HEADS).astype(jnp.float32)


def spiked(values, rng, source, target, blocks, factor):
    def block_of(dim):
        return (jnp.arange(values.shape[dim]) // (values.shape[dim] // blocks)).reshape((-1,) + (1,) * (values.ndim - 1 - dim))

    near = jax.random.permutation(rng, blocks)[block_of(target)]
    far = (block_of(target) + blocks // 2) % blocks
    return jnp.where((block_of(source) == near) | (block_of(source) == far), factor * values, values)


def block_levels(own_key, shape, cuts, low, high):
    def one(axis_at, shards_of):
        draws = jax.random.uniform(jax.random.fold_in(jax.random.fold_in(own_key, 6), axis_at), (shards_of,), jnp.float32, low / len(cuts), high / len(cuts))
        return jnp.repeat(jnp.exp(draws), shape[axis_at] // shards_of).reshape((-1,) + (1,) * (len(shape) - axis_at - 1))

    gain = one(*cuts[0])
    for cut in cuts[1:]:
        gain = gain * one(*cut)
    return gain


def scatter_about(stream_key, extent, spread, reach, cuts=(), dtype=jnp.bfloat16):
    drawn = spread * jax.random.normal(stream_key, extent, jnp.float32)
    if cuts:
        drawn = drawn * block_levels(stream_key, extent, cuts, -0.22, 0.18)
    return jnp.clip(drawn, -reach, reach).astype(dtype)


def bell_draw_with(own_key, dims, spread, bound, shards, heavy, held_as=jnp.bfloat16):
    drawn = spread * jax.random.normal(own_key, dims, jnp.float32)
    if shards:
        drawn = drawn * block_levels(own_key, dims, shards, -0.22, 0.18)
    return jnp.clip(spiked(drawn, jax.random.fold_in(own_key, 3), *heavy), -bound, bound).astype(held_as)


def setup_inputs(seed: int = 0) -> dict:
    streams_of = jax.random.split(jax.random.key(seed), 8)
    return {
        "layer_input": bell_draw_with(streams_of[0], (N_ISLAND, N_DP, SEQUENCE_LENGTH, D), 1.0, 6.0, ((0, 16), (1, 8), (2, 2)), (2, 3, 2, 2.0)),
        "inner_acts": scatter_about(streams_of[1], (N_ISLAND, N_DP, SEQUENCE_LENGTH, HP), 1.0, 6.0, ((0, 16), (1, 8), (2, 2))),
        "out_grad": scatter_about(streams_of[2], (N_ISLAND, N_DP, SEQUENCE_LENGTH, HP), 1.0, 6.0, ((0, 16), (1, 8), (2, 2))),
        "step_sizes": draw_step_sizes(jax.random.fold_in(streams_of[7], 71), 0),
        "outer_weight": scatter_about(streams_of[4], (D, 2 * STATE), 1.0, 6.0, ((0, 16),), jnp.float32),
        "island_drift": scatter_about(streams_of[5], (N_ISLAND, D, 2 * STATE), 1.0, 6.0, ((0, 16), (1, 16)), jnp.float32),
        "momentum": scatter_about(streams_of[6], (D, 2 * STATE), 1.0, 6.0, ((0, 16),), jnp.float32),
    }


HIGH = lax.Precision.HIGHEST

def block_decays(step_block):
    levels = jnp.cumsum(step_block, axis=0)
    finals = levels[-1]
    entry_decay = jnp.exp(-levels)
    exit_weight = step_block * jnp.exp(levels - finals[None, :])
    return (levels, finals, entry_decay, exit_weight)

def block_summary(inner_block, grad_block, step_block, sel_block):
    rows_here = step_block.shape[0]
    levels, finals, entry_decay, exit_weight = block_decays(step_block)
    inner_heads = inner_block.reshape(rows_here, LOCAL_HEADS, HEAD_DIM).astype(jnp.float32)
    grad_heads = grad_block.reshape(rows_here, LOCAL_HEADS, HEAD_DIM).astype(jnp.float32)
    input_map = sel_block[:, :STATE].astype(jnp.float32)
    output_map = sel_block[:, STATE:].astype(jnp.float32)
    shrink = jnp.exp(-finals)
    produced = jnp.einsum('sn,shp->hnp', input_map, inner_heads * exit_weight[:, :, None], precision=HIGH)
    received = jnp.einsum('rn,rhp->hnp', output_map, grad_heads * entry_decay[:, :, None], precision=HIGH)
    return (shrink, produced, received)

def block_grads(inner_block, grad_block, step_block, sel_block, state_in, adjoint_out):
    rows_here = step_block.shape[0]
    levels, finals, entry_decay, exit_weight = block_decays(step_block)
    inner_f = inner_block.reshape(rows_here, LOCAL_HEADS, HEAD_DIM).astype(jnp.float32)
    grad_f = grad_block.reshape(rows_here, LOCAL_HEADS, HEAD_DIM).astype(jnp.float32)
    input_map = sel_block[:, :STATE].astype(jnp.float32)
    output_map = sel_block[:, STATE:].astype(jnp.float32)
    spans = levels.T[:, :, None] - levels.T[:, None, :]
    token_positions = jnp.arange(rows_here)
    lower = token_positions[:, None] >= token_positions[None, :]
    within = jnp.exp(-jnp.where(lower[None, :, :], spans, jnp.inf))
    scores = jnp.einsum('thp,shp->hts', grad_f, inner_f, precision=HIGH)
    mixing = lax.optimization_barrier(jnp.sum(within * scores * step_block.T[:, None, :], axis=0))
    intersection = jnp.dot(sel_block[:, STATE:], sel_block[:, :STATE].T, preferred_element_type=jnp.float32)
    d_input = jnp.dot(mixing.T, output_map, precision=HIGH) + jnp.einsum('shp,hnp->sn', inner_f * exit_weight[:, :, None], adjoint_out, precision=HIGH)
    d_output = jnp.dot(mixing, input_map, precision=HIGH) + jnp.einsum('thp,hnp->tn', grad_f * entry_decay[:, :, None], state_in, precision=HIGH)
    local_part = jnp.einsum('hrs,rhp->shp', within * intersection[None, :, :], grad_f, precision=HIGH)
    carried = jnp.einsum('sn,hnp->shp', input_map, adjoint_out, precision=HIGH)
    in_grad = (step_block[:, :, None] * local_part + exit_weight[:, :, None] * carried).reshape(rows_here, LOCAL_HEADS * HEAD_DIM)
    sel_grad = jnp.concatenate([d_input, d_output], axis=1)
    return (in_grad.astype(jnp.bfloat16), sel_grad.astype(jnp.bfloat16))

def sequence_grads(inputs_row, inner_row, grad_row, step_row, weight_copy):
    sel_row = (jnp.dot(inputs_row, weight_copy, preferred_element_type=jnp.float32) / math.sqrt(D)).astype(jnp.bfloat16)
    blocks = SEQUENCE_LENGTH // T_DEV

    def to_blocks(values):
        return values.reshape((blocks, T_DEV) + values.shape[1:])
    inner_blocks = to_blocks(inner_row)
    grad_blocks = to_blocks(grad_row)
    step_blocks = to_blocks(step_row)
    sel_blocks = to_blocks(sel_row)
    shrinks, produced, received = lax.map(lambda pieces: block_summary(*pieces), (inner_blocks, grad_blocks, step_blocks, sel_blocks))
    zero_state = jnp.zeros((LOCAL_HEADS, STATE, HEAD_DIM), jnp.float32)

    def forward(carried_state, pieces):
        return (pieces[0][:, None, None] * carried_state + pieces[1], carried_state)

    def backward(adjoint, pieces):
        return (pieces[1] + pieces[0][:, None, None] * adjoint, adjoint)
    _, states_in = lax.scan(forward, zero_state, (shrinks, produced))
    _, adjoints_out = lax.scan(backward, zero_state, (shrinks, received), reverse=True)
    in_grads, sel_grads = lax.map(lambda pieces: block_grads(*pieces), (inner_blocks, grad_blocks, step_blocks, sel_blocks, states_in, adjoints_out))
    sel_flat = sel_grads.reshape(SEQUENCE_LENGTH, 2 * STATE)
    weight_grad = jnp.dot(inputs_row.T, sel_flat, preferred_element_type=jnp.float32)
    return (in_grads.reshape(SEQUENCE_LENGTH, LOCAL_HEADS * HEAD_DIM), sel_flat, weight_grad)

def reference(layer_input, inner_acts, out_grad, step_sizes, outer_weight, island_drift, momentum):

    def island_work(pieces):
        inputs_isl, inner_isl, grad_isl, step_isl, drift_rows = pieces
        weight_copy = (outer_weight + drift_rows).astype(jnp.bfloat16)
        in_grads, sel_grads, weight_grads = lax.map(lambda member: sequence_grads(member[0], member[1], member[2], member[3], weight_copy), (inputs_isl, inner_isl, grad_isl, step_isl))
        pseudo = 0.5 * (lax.optimization_barrier(jnp.sum(weight_grads, axis=0)) / math.sqrt(D)) - drift_rows
        return (in_grads, sel_grads, pseudo)
    in_grad, sel_grad, pseudo = lax.map(island_work, (layer_input, inner_acts, out_grad, step_sizes, island_drift))
    outer_delta = lax.optimization_barrier(jnp.mean(pseudo, axis=0))
    new_momentum = 0.9 * momentum + outer_delta
    new_outer = outer_weight - 0.7 * (outer_delta + 0.9 * new_momentum)
    return (in_grad, sel_grad, new_momentum, new_outer)
```

```python
import functools
import math

import jax
import jax.numpy as jnp
from jax import lax
from jax.experimental import pallas as pl
from jax.experimental.pallas import tpu as pltpu
from jax.sharding import PartitionSpec as P

MESH = pl.DeviceIdType.MESH
BF = jnp.bfloat16
F32 = jnp.float32
HEADS = 128
T = 128
NZ = 8
NQ = 4
VMEM_LIMIT = 50 * 1024 * 1024


def dot(a, b, ca=1, cb=0):
    return lax.dot_general(a, b, (((ca,), (cb,)), ((), ())), preferred_element_type=F32)


def remote(src, dst, send, recv, device):
    return pltpu.make_async_remote_copy(
        src_ref=src, dst_ref=dst, send_sem=send, recv_sem=recv, device_id=device, device_id_type=MESH
    )


def kernel(
    x_hbm, ia_hbm, dy_hbm, dt_hbm, ow_hbm, dr_hbm,
    ig_hbm, sg_hbm, delta_hbm,
    ow, dr, dt, ia, dy, wg, xs, xr, xt, ds16, dr16,
    lq, lt, mixacc, ew, pw, ewx, gw, e_all, ig, mb, mt2, m2,
    psel, prem, sel, sall, gf, gs, r2, t2, t2b, r3, dl,
    loc, ring_s, ring_r, pair_s, pair_r, xr_s, xr_r, dr_s, dr_r,
    s_s, s_r, p_s, p_r, z_s, z_r, a_s, a_r, b_s, b_r, outs,
):
    s = lax.axis_index("seq")
    z = lax.axis_index("dp")
    isl = lax.axis_index("island")
    y = isl // 4
    x = isl % 4
    p1 = x + s * (y - x)
    p2 = y + s * (x - y)
    base1 = (1 - s) * 4 * y + s * x
    mul1 = 1 + 3 * s
    base2 = (1 - s) * x + s * 4 * y
    mul2 = 4 - 3 * s

    def first(k):
        return {"seq": s, "dp": z, "island": base1 + mul1 * ((p1 + k) % 4)}

    def second(k):
        return {"seq": s, "dp": z, "island": base2 + mul2 * ((p2 + k) % 4)}

    def along(k):
        return {"seq": s, "dp": (z + k) % 8, "island": isl}

    partner = {"seq": 1 - s, "dp": z, "island": isl}

    c_ow = pltpu.make_async_copy(ow_hbm, ow, loc.at[0])
    c_dr = pltpu.make_async_copy(dr_hbm, dr, loc.at[1])
    c_dt = pltpu.make_async_copy(dt_hbm, dt, loc.at[2])
    c_ia = pltpu.make_async_copy(ia_hbm, ia, loc.at[3])
    c_dy = pltpu.make_async_copy(dy_hbm, dy, loc.at[4])
    for c in (c_ow, c_dr, c_dt, c_dy, c_ia):
        c.start()

    def load_x(c, carry):
        col = pl.multiple_of(s * 4096 + c * 128, 128)
        pltpu.make_async_copy(
            x_hbm.at[:, pl.ds(col, 128)], xs.at[c % 4, c // 4, pl.ds(pl.multiple_of(s * T, T), T)], loc.at[5]
        ).start()
        return carry

    lax.fori_loop(0, 32, load_x, 0)

    barrier = pltpu.get_barrier_semaphore()
    peers = [partner] + [along(k) for k in range(1, 8)] + [first(k) for k in range(1, 4)] + [second(k) for k in range(1, 4)]
    for d in peers:
        pl.semaphore_signal(barrier, inc=1, device_id=d, device_id_type=MESH)

    c_ow.wait()
    c_dr.wait()
    wg[z] = (ow[...] + dr[...]).astype(BF)
    for q in range(4):
        ds16[q] = dr[pl.ds(q * 128, 128), :].astype(BF)

    pl.semaphore_wait(barrier, len(peers))

    def right(j, zb, half):
        at = wg.at[zb, pl.ds(pl.multiple_of(half * 256, 256), 256)]
        return remote(at, at, ring_s.at[0, j], ring_r.at[0, j], along(1))

    def left(j, zb, half):
        at = wg.at[zb, pl.ds(pl.multiple_of(half * 256, 256), 256)]
        return remote(at, at, ring_s.at[1, j], ring_r.at[1, j], along(7))

    right(0, z, 0).start()
    left(0, z, 1).start()
    right(1, z, 1).start()
    left(1, z, 0).start()

    def send_x(c, carry):
        col = pl.multiple_of((1 - s) * 4096 + c * 128, 128)
        remote(
            x_hbm.at[:, pl.ds(col, 128)], xs.at[c % 4, c // 4, pl.ds(pl.multiple_of(s * T, T), T)],
            pair_s.at[0], pair_r.at[0], partner,
        ).start()
        return carry

    lax.fori_loop(0, 32, send_x, 0)

    c_dt.wait()
    rows = lax.broadcasted_iota(jnp.int32, (T, T), 0)
    cols = lax.broadcasted_iota(jnp.int32, (T, T), 1)
    tri = (rows >= cols).astype(F32)
    steps = dt[...]
    levels = lax.dot_general(
        tri, steps, (((1,), (0,)), ((), ())), precision=lax.Precision.HIGHEST, preferred_element_type=F32
    )
    finals = levels[T - 1 : T, :]
    logs = jnp.where(steps > 0.0, jnp.log(jnp.where(steps > 0.0, steps, 1.0)), -1e30)
    lq[...] = levels + logs
    lt[...] = levels.T
    first_core = s == 0
    factor = jnp.exp(jnp.where(first_core, (levels - finals) + logs, -levels))
    hi = factor.astype(BF)
    ew[:, 0:T] = hi
    ew[:, T : 2 * T] = (factor - hi.astype(F32)).astype(BF)
    c_ia.wait()
    c_dy.wait()

    def widen(c, carry):
        wide = 512
        kk = lax.broadcasted_iota(jnp.int32, (2 * T, wide), 0)
        ll = lax.broadcasted_iota(jnp.int32, (2 * T, wide), 1)
        spread = ((kk % T) == c * 8 + ll // 64).astype(F32).astype(BF)
        fac = dot(ew[...], spread)
        off = pl.ds(pl.multiple_of(c * wide, wide), wide)
        ewx[:, off] = fac.astype(BF)

        @pl.when(s == 0)
        def _():
            pw[:, off] = (ia[:, off].astype(F32) * fac).astype(BF)

        @pl.when(s == 1)
        def _():
            gw[:, off] = (dy[:, off].astype(F32) * fac).astype(BF)

        return carry

    lax.fori_loop(0, 16, widen, 0)

    c_gw = remote(gw, gw, pair_s.at[1], pair_r.at[1], partner)

    @pl.when(s == 1)
    def _():
        c_gw.start()

    own_x = xs.at[:, :, pl.ds(pl.multiple_of(s * T, T), T)]
    pltpu.make_async_copy(own_x, own_x, loc.at[5]).wait()
    other_x = xs.at[:, :, pl.ds(pl.multiple_of((1 - s) * T, T), T)]
    remote(own_x, other_x, pair_s.at[0], pair_r.at[0], partner).wait_recv()
    for k in range(1, 4):
        remote(xs.at[(p1 + k) % 4], xr.at[k - 1], xr_s.at[k - 1], xr_r.at[k - 1], first(k)).start()
        remote(ds16.at[(p1 + k) % 4], dr16.at[k - 1], dr_s.at[k - 1], dr_r.at[k - 1], first(k)).start()

    mixacc[...] = jnp.zeros((T, T), F32)
    low = lax.broadcasted_iota(jnp.int32, (T, T), 1) < 64
    keep = rows <= cols
    none = jnp.zeros((T, T), BF)

    def group(g):
        shifted = pltpu.roll(lq[...], (128 - 8 * g) % 128, 1)
        lrow = lt[pl.ds(pl.multiple_of(8 * g, 8), 8), :]
        mix = mixacc[...]
        for pair in range(4):
            off = pl.ds(pl.multiple_of(g * 512 + pair * 128, 128), 128)
            xp = ia[:, off]
            both = jnp.concatenate([jnp.where(low, xp, none), jnp.where(low, none, xp)], axis=0)
            scores = dot(both, dy[:, off], 1, 1)
            for u in range(2):
                c = 2 * pair + u
                e = jnp.where(keep, jnp.exp(shifted[:, c : c + 1] - lrow[c : c + 1, :]), 0.0)
                mix = mix + e * scores[u * T : (u + 1) * T, :]
                e_all[g * 8 + c] = e.astype(BF)
        mixacc[...] = mix

    def partial_sel(zb, half):
        a = jnp.concatenate([xs[2 * half, zb], xs[2 * half + 1, zb]], axis=1)
        return dot(a, wg[zb, pl.ds(pl.multiple_of(half * 256, 256), 256), :])

    psel[...] = partial_sel(z, 0) + partial_sel(z, 1)
    group(14)
    group(15)

    def event(j, carry):
        k = j // 2 + 1
        hr = j % 2
        hl = 1 - hr
        zr = (z - k + 8) % 8
        zl = (z + k) % 8
        right(j, zr, hr).wait_recv()

        @pl.when(j < 5)
        def _():
            right(j + 2, zr, hr).start()

        left(j, zl, hl).wait_recv()

        @pl.when(j < 5)
        def _():
            left(j + 2, zl, hl).start()

        psel[...] += partial_sel(zr, hr) + partial_sel(zl, hl)

        @pl.when(j < 6)
        def _():
            group(2 * j)
            group(2 * j + 1)

        return carry

    group(12)
    group(13)
    lax.fori_loop(0, 7, event, 0)

    c_psel = remote(psel, prem, pair_s.at[2], pair_r.at[2], partner)
    c_psel.start()

    c_mb0 = remote(mb.at[pl.ds(0, 2)], mb.at[pl.ds(0, 2)], pair_s.at[3], pair_r.at[3], partner)
    c_mb1 = remote(mb.at[2], mb.at[2], pair_s.at[4], pair_r.at[4], partner)

    @pl.when(s == 0)
    def _():
        c_gw.wait_recv()
        mb[0] = mixacc[...]
        mb[1] = dot(pw[...], gw[...], 1, 1)
        c_mb0.start()
        c_mb1.wait_recv()

    @pl.when(s == 1)
    def _():
        mb[2] = mixacc[...]
        c_mb1.start()
        c_mb0.wait_recv()

    mt = jnp.concatenate(
        [jnp.concatenate([mb[0], mb[1]], axis=1), jnp.concatenate([jnp.zeros((T, T), F32), mb[2]], axis=1)], axis=0
    )
    mth = mt.astype(BF)
    mt2[0] = mth
    mt2[1] = (mt - mth.astype(F32)).astype(BF)
    m = mt.T
    mh = m.astype(BF)
    m2[0] = mh
    m2[1] = (m - mh.astype(F32)).astype(BF)

    def turn_own(zb, carry):
        xt[zb, :, 0:256] = xs[p1, zb].T
        return carry

    lax.fori_loop(0, 8, turn_own, 0)
    for k in range(1, 4):
        remote(xs.at[(p1 + k) % 4], xr.at[k - 1], xr_s.at[k - 1], xr_r.at[k - 1], first(k)).wait_recv()

        def turn(zb, carry):
            xt[zb, :, k * 256 : (k + 1) * 256] = xr[k - 1, zb].T
            return carry

        lax.fori_loop(0, 8, turn, 0)
        remote(ds16.at[(p1 + k) % 4], dr16.at[k - 1], dr_s.at[k - 1], dr_r.at[k - 1], first(k)).wait_recv()

    c_psel.wait_recv()
    sel[...] = ((psel[...] + prem[...]) * (1.0 / math.sqrt(8192.0))).astype(BF)
    bmap = sel[:, 0:T]
    cmap = sel[:, T : 2 * T]
    d_in = dot(mt2[0], cmap) + dot(mt2[1], cmap)
    d_out = dot(m2[0], bmap) + dot(m2[1], bmap)
    sall[0] = jnp.concatenate([d_in, d_out], axis=1).astype(BF)
    for k in range(1, 4):
        remote(sall.at[0], sall.at[k], s_s.at[k - 1], s_r.at[k - 1], first(k)).start()
    c_sg = pltpu.make_async_copy(sall.at[0, pl.ds(pl.multiple_of(s * T, T), T)], sg_hbm, outs.at[0])
    c_sg.start()

    mine = pl.ds(pl.multiple_of(s * T, T), T)
    inter = dot(sel[mine, 0:T], sel[mine, T : 2 * T], 1, 1).astype(BF)
    across = (dot(sel[0:T, 0:T], sel[T : 2 * T, T : 2 * T], 1, 1) * (1 - s).astype(F32)).astype(BF)

    def grads(start, stop):
        def one(j, carry):
            off = pl.ds(pl.multiple_of(j * 128, 128), 128)
            dp = dy[:, off]
            lhs = jnp.concatenate([e_all[2 * j] * inter, e_all[2 * j + 1] * inter], axis=1)
            rhs = jnp.concatenate([jnp.where(low, dp, none), jnp.where(low, none, dp)], axis=0)
            out = dot(lhs, rhs) + ewx[:, off].astype(F32) * dot(across, gw[:, off])
            ig[:, off] = out.astype(BF)
            return carry

        lax.fori_loop(start, stop, one, 0)

    grads(0, 24)

    for k in range(1, 4):
        remote(sall.at[0], sall.at[k], s_s.at[k - 1], s_r.at[k - 1], first(k)).wait_recv()

    scale = 0.5 / math.sqrt(8192.0)

    def weight(zb, carry):
        gf[zb] = dot(xt[zb], sall[...].reshape(1024, 256)) * scale
        return carry

    lax.fori_loop(0, 8, weight, 0)
    drift = dr[pl.ds(pl.multiple_of(p1 * 128, 128), 128), :]
    for k in range(3):
        drift = drift + dr16[k].astype(F32)
    gf[z] = gf[z] - drift
    for q in range(4):
        gs[q] = gf[:, q * 32 : (q + 1) * 32, :].astype(BF)
    for k in range(1, 4):
        remote(gs.at[(p2 + k) % 4], r2.at[k - 1], p_s.at[k - 1], p_r.at[k - 1], second(k)).start()
    grads(24, 40)
    total = gf[:, pl.ds(pl.multiple_of(p2 * 32, 32), 32), :]
    for k in range(1, 4):
        remote(gs.at[(p2 + k) % 4], r2.at[k - 1], p_s.at[k - 1], p_r.at[k - 1], second(k)).wait_recv()
        total = total + r2[k - 1].astype(F32)
    t2[...] = total
    t2b[...] = total.astype(BF)
    for k in range(1, 8):
        remote(t2b.at[(z + k) % 8], r3.at[k - 1], z_s.at[k - 1], z_r.at[k - 1], along(k)).start()
    grads(40, 52)
    part = t2[z]
    for k in range(1, 8):
        remote(t2b.at[(z + k) % 8], r3.at[k - 1], z_s.at[k - 1], z_r.at[k - 1], along(k)).wait_recv()
        part = part + r3[k - 1].astype(F32)
    dl[p1, p2] = (part * (1.0 / 16.0)).astype(BF)
    for k in range(1, 4):
        remote(dl.at[p1, p2], dl.at[p1, p2], a_s.at[k - 1], a_r.at[k - 1], second(k)).start()
    grads(52, 58)
    for k in range(1, 4):
        at = dl.at[p1, (p2 + 4 - k) % 4]
        remote(at, at, a_s.at[k - 1], a_r.at[k - 1], second(k)).wait_recv()
    for k in range(1, 4):
        remote(dl.at[p1], dl.at[p1], b_s.at[k - 1], b_r.at[k - 1], first(k)).start()
    grads(58, 64)
    c_ig = pltpu.make_async_copy(ig, ig_hbm, outs.at[1])
    c_ig.start()
    for k in range(1, 4):
        at = dl.at[(p1 + 4 - k) % 4]
        remote(at, at, b_s.at[k - 1], b_r.at[k - 1], first(k)).wait_recv()
    c_delta = pltpu.make_async_copy(dl, delta_hbm, outs.at[2])
    c_delta.start()

    def drain(j, carry):
        right(j, z, 0).wait_send()
        left(j, z, 0).wait_send()
        return carry

    lax.fori_loop(0, 7, drain, 0)
    remote(own_x, other_x, pair_s.at[0], pair_r.at[0], partner).wait_send()
    c_psel.wait_send()

    @pl.when(s == 0)
    def _():
        c_mb0.wait_send()

    @pl.when(s == 1)
    def _():
        c_gw.wait_send()
        c_mb1.wait_send()

    for k in range(1, 4):
        remote(xs.at[0], xr.at[k - 1], xr_s.at[k - 1], xr_r.at[k - 1], first(k)).wait_send()
        remote(ds16.at[0], dr16.at[k - 1], dr_s.at[k - 1], dr_r.at[k - 1], first(k)).wait_send()
        remote(sall.at[0], sall.at[k], s_s.at[k - 1], s_r.at[k - 1], first(k)).wait_send()
        remote(gs.at[0], r2.at[k - 1], p_s.at[k - 1], p_r.at[k - 1], second(k)).wait_send()
        remote(dl.at[p1, p2], dl.at[p1, p2], a_s.at[k - 1], a_r.at[k - 1], second(k)).wait_send()
        remote(dl.at[p1], dl.at[p1], b_s.at[k - 1], b_r.at[k - 1], first(k)).wait_send()
    for k in range(1, 8):
        remote(t2b.at[0], r3.at[k - 1], z_s.at[k - 1], z_r.at[k - 1], along(k)).wait_send()
    c_sg.wait()
    c_ig.wait()
    c_delta.wait()


def local(layer_input, inner_acts, out_grad, step_sizes, outer_weight, island_drift, momentum):
    anyspec = pl.BlockSpec(memory_space=pl.ANY)
    dma = pltpu.SemaphoreType.DMA
    vm = pltpu.VMEM
    in_grad, sel_grad, delta = pl.pallas_call(
        kernel,
        out_shape=(
            jax.ShapeDtypeStruct((T, 8192), BF),
            jax.ShapeDtypeStruct((T, 256), BF),
            jax.ShapeDtypeStruct((4, 4, 32, 256), BF),
        ),
        in_specs=[anyspec] * 6,
        out_specs=(anyspec, anyspec, anyspec),
        scratch_shapes=[
            vm((512, 256), F32),
            vm((512, 256), F32),
            vm((T, HEADS), F32),
            vm((T, 8192), BF),
            vm((T, 8192), BF),
            vm((8, 512, 256), BF),
            vm((4, 8, 256, 128), BF),
            vm((3, 8, 256, 128), BF),
            vm((8, 128, 1024), BF),
            vm((4, 128, 256), BF),
            vm((3, 128, 256), BF),
            vm((T, HEADS), F32),
            vm((HEADS, T), F32),
            vm((T, T), F32),
            vm((T, 2 * T), BF),
            vm((T, 8192), BF),
            vm((T, 8192), BF),
            vm((T, 8192), BF),
            vm((HEADS, T, T), BF),
            vm((T, 8192), BF),
            vm((3, T, T), F32),
            vm((2, 256, 256), BF),
            vm((2, 256, 256), BF),
            vm((256, 256), F32),
            vm((256, 256), F32),
            vm((256, 256), BF),
            vm((4, 256, 256), BF),
            vm((8, 128, 256), F32),
            vm((4, 8, 32, 256), BF),
            vm((3, 8, 32, 256), BF),
            vm((8, 32, 256), F32),
            vm((8, 32, 256), BF),
            vm((7, 32, 256), BF),
            vm((4, 4, 32, 256), BF),
            dma((6,)),
            dma((2, 7)),
            dma((2, 7)),
            dma((5,)),
            dma((5,)),
            dma((3,)), dma((3,)),
            dma((3,)), dma((3,)),
            dma((3,)), dma((3,)),
            dma((3,)), dma((3,)),
            dma((7,)), dma((7,)),
            dma((3,)), dma((3,)),
            dma((3,)), dma((3,)),
            dma((3,)),
        ],
        compiler_params=pltpu.CompilerParams(
            collective_id=0, has_side_effects=True, vmem_limit_bytes=VMEM_LIMIT
        ),
    )(
        layer_input[0, 0], inner_acts[0, 0], out_grad[0, 0], step_sizes[0, 0], outer_weight, island_drift[0]
    )
    outer_delta = delta.reshape(512, 256).astype(F32)
    new_momentum = 0.9 * momentum + outer_delta
    new_outer = outer_weight - 0.7 * (outer_delta + 0.9 * new_momentum)
    return (in_grad[None, None], sel_grad[None, None], new_momentum, new_outer)


def solution(mesh):
    acts = P("island", "dp", "seq", None)
    rows = P(("seq", "dp"), None)
    return jax.shard_map(
        local,
        mesh=mesh,
        in_specs=(acts, acts, acts, acts, rows, P("island", ("seq", "dp"), None), rows),
        out_specs=(acts, acts, rows, rows),
        check_vma=False,
    )
```

```python
import functools
import math

import jax
import jax.numpy as jnp
from jax import lax
from jax.experimental import pallas as pl
from jax.experimental.pallas import tpu as pltpu
from jax.sharding import PartitionSpec as P

MESH = pl.DeviceIdType.MESH
BF = jnp.bfloat16
F32 = jnp.float32
HEADS = 128
T = 128
NZ = 8
NQ = 4
EVENTS = 14
VMEM_LIMIT = 60 * 1024 * 1024
FINISH_LIMIT = 62 * 1024 * 1024


def dot(a, b, ca=1, cb=0):
    return lax.dot_general(a, b, (((ca,), (cb,)), ((), ())), preferred_element_type=F32)


def remote(src, dst, send, recv, device):
    return pltpu.make_async_remote_copy(
        src_ref=src, dst_ref=dst, send_sem=send, recv_sem=recv, device_id=device, device_id_type=MESH
    )


def kernel(
    x_hbm, ia_hbm, dy_hbm, dt_hbm, ow_hbm, dr_hbm,
    ig_hbm, sg_hbm, delta_hbm,
    ow, dr, dt, ia, dy, wg, xs, xr, xt, ds16, dr16,
    lq, lt, mixacc, ew, pw, ewx, gw, e_all, ig, mb, mt2, m2,
    psel, prem, sel, sall, gf, gs, r2, t2, t2b, r3, dl,
    loc, ring_s, ring_r, pair_s, pair_r, xr_s, xr_r, dr_s, dr_r,
    s_s, s_r, p_s, p_r, z_s, z_r, a_s, a_r, outs,
):
    s = lax.axis_index("seq")
    z = lax.axis_index("dp")
    isl = lax.axis_index("island")
    y = isl // 4
    x = isl % 4
    p1 = x + s * (y - x)
    p2 = y + s * (x - y)
    base1 = (1 - s) * 4 * y + s * x
    mul1 = 1 + 3 * s
    base2 = (1 - s) * x + s * 4 * y
    mul2 = 4 - 3 * s

    def first(k):
        return {"seq": s, "dp": z, "island": base1 + mul1 * ((p1 + k) % 4)}

    def second(k):
        return {"seq": s, "dp": z, "island": base2 + mul2 * ((p2 + k) % 4)}

    def along(k):
        return {"seq": s, "dp": (z + k) % 8, "island": isl}

    partner = {"seq": 1 - s, "dp": z, "island": isl}

    c_ow = pltpu.make_async_copy(ow_hbm, ow, loc.at[0])
    c_dr = pltpu.make_async_copy(dr_hbm, dr, loc.at[1])
    c_dt = pltpu.make_async_copy(dt_hbm, dt, loc.at[2])
    c_ia = pltpu.make_async_copy(ia_hbm, ia, loc.at[3])
    c_dy = pltpu.make_async_copy(dy_hbm, dy, loc.at[4])
    for c in (c_ow, c_dr, c_dt, c_dy, c_ia):
        c.start()

    def load_x(c, carry):
        col = pl.multiple_of(s * 4096 + c * 128, 128)
        pltpu.make_async_copy(
            x_hbm.at[:, pl.ds(col, 128)], xs.at[c % 4, c // 4, pl.ds(pl.multiple_of(s * T, T), T)], loc.at[5]
        ).start()
        return carry

    lax.fori_loop(0, 32, load_x, 0)

    barrier = pltpu.get_barrier_semaphore()
    peers = [partner] + [along(k) for k in range(1, 8)]
    peers += [{"seq": s, "dp": z, "island": (isl + k) % 16} for k in range(1, 16)]
    for d in peers:
        pl.semaphore_signal(barrier, inc=1, device_id=d, device_id_type=MESH)

    c_ow.wait()
    c_dr.wait()
    wg[z] = (ow[...] + dr[...]).astype(BF).reshape(4, 128, 256)
    for q in range(4):
        ds16[q] = dr[pl.ds(q * 128, 128), :].astype(BF)

    pl.semaphore_wait(barrier, len(peers))

    def right(j, zb, q):
        at = wg.at[zb, q]
        return remote(at, at, ring_s.at[0, j], ring_r.at[0, j], along(1))

    def left(j, zb, q):
        at = wg.at[zb, q]
        return remote(at, at, ring_s.at[1, j], ring_r.at[1, j], along(7))

    for j in range(4):
        right(j, z, j).start()
        left(j, z, 3 - j).start()

    def send_x(c, carry):
        col = pl.multiple_of((1 - s) * 4096 + c * 128, 128)
        remote(
            x_hbm.at[:, pl.ds(col, 128)], xs.at[c % 4, c // 4, pl.ds(pl.multiple_of(s * T, T), T)],
            pair_s.at[0], pair_r.at[0], partner,
        ).start()
        return carry

    lax.fori_loop(0, 32, send_x, 0)

    c_dt.wait()
    rows = lax.broadcasted_iota(jnp.int32, (T, T), 0)
    cols = lax.broadcasted_iota(jnp.int32, (T, T), 1)
    tri = (rows >= cols).astype(F32)
    steps = dt[...]
    levels = lax.dot_general(
        tri, steps, (((1,), (0,)), ((), ())), precision=lax.Precision.HIGHEST, preferred_element_type=F32
    )
    finals = levels[T - 1 : T, :]
    logs = jnp.where(steps > 0.0, jnp.log(jnp.where(steps > 0.0, steps, 1.0)), -1e30)
    lq[...] = levels + logs
    lt[...] = levels.T
    first_core = s == 0
    factor = jnp.exp(jnp.where(first_core, (levels - finals) + logs, -levels))
    hi = factor.astype(BF)
    ew[:, 0:T] = hi
    ew[:, T : 2 * T] = (factor - hi.astype(F32)).astype(BF)
    c_ia.wait()
    c_dy.wait()

    def widen(c, carry):
        wide = 512
        kk = lax.broadcasted_iota(jnp.int32, (2 * T, wide), 0)
        ll = lax.broadcasted_iota(jnp.int32, (2 * T, wide), 1)
        spread = ((kk % T) == c * 8 + ll // 64).astype(F32).astype(BF)
        fac = dot(ew[...], spread)
        off = pl.ds(pl.multiple_of(c * wide, wide), wide)
        ewx[:, off] = fac.astype(BF)

        @pl.when(s == 0)
        def _():
            pw[:, off] = (ia[:, off].astype(F32) * fac).astype(BF)

        @pl.when(s == 1)
        def _():
            gw[:, off] = (dy[:, off].astype(F32) * fac).astype(BF)

        return carry

    lax.fori_loop(0, 16, widen, 0)

    c_gw = remote(gw, gw, pair_s.at[1], pair_r.at[1], partner)

    @pl.when(s == 1)
    def _():
        c_gw.start()

    own_x = xs.at[:, :, pl.ds(pl.multiple_of(s * T, T), T)]
    pltpu.make_async_copy(own_x, own_x, loc.at[5]).wait()
    other_x = xs.at[:, :, pl.ds(pl.multiple_of((1 - s) * T, T), T)]
    remote(own_x, other_x, pair_s.at[0], pair_r.at[0], partner).wait_recv()
    for k in range(1, 4):
        remote(xs.at[(p1 + k) % 4], xr.at[k - 1], xr_s.at[k - 1], xr_r.at[k - 1], first(k)).start()
        remote(ds16.at[(p1 + k) % 4], dr16.at[k - 1], dr_s.at[k - 1], dr_r.at[k - 1], first(k)).start()

    mixacc[...] = jnp.zeros((T, T), F32)
    low = lax.broadcasted_iota(jnp.int32, (T, T), 1) < 64
    keep = rows <= cols
    none = jnp.zeros((T, T), BF)

    def group(g):
        shifted = pltpu.roll(lq[...], (128 - 8 * g) % 128, 1)
        lrow = lt[pl.ds(pl.multiple_of(8 * g, 8), 8), :]
        mix = mixacc[...]
        for pair in range(4):
            off = pl.ds(pl.multiple_of(g * 512 + pair * 128, 128), 128)
            xp = ia[:, off]
            both = jnp.concatenate([jnp.where(low, xp, none), jnp.where(low, none, xp)], axis=0)
            scores = dot(both, dy[:, off], 1, 1)
            for u in range(2):
                c = 2 * pair + u
                e = jnp.where(keep, jnp.exp(shifted[:, c : c + 1] - lrow[c : c + 1, :]), 0.0)
                mix = mix + e * scores[u * T : (u + 1) * T, :]
                e_all[g * 8 + c] = e.astype(BF)
        mixacc[...] = mix

    def two_parts(za, qa, zb, qb):
        a = jnp.concatenate([xs[qa, za], xs[qb, zb]], axis=1)
        b = jnp.concatenate([wg[za, qa], wg[zb, qb]], axis=0)
        return dot(a, b)

    def event(j, forward):
        k = j // 4 + 1
        qr = j % 4
        ql = 3 - qr
        zr = (z - k + 8) % 8
        zl = (z + k) % 8
        right(j, zr, qr).wait_recv()
        if forward:
            right(j + 4, zr, qr).start()
        left(j, zl, ql).wait_recv()
        if forward:
            left(j + 4, zl, ql).start()
        psel[...] += two_parts(zr, qr, zl, ql)

    psel[...] = two_parts(z, 0, z, 1) + two_parts(z, 2, z, 3)
    group(0)
    group(1)

    def busy(j, carry):
        event(j, True)
        group(2 * j + 2)
        group(2 * j + 3)
        return carry

    lax.fori_loop(0, 7, busy, 0)

    c_mb0 = remote(mb.at[pl.ds(0, 2)], mb.at[pl.ds(0, 2)], pair_s.at[3], pair_r.at[3], partner)
    c_mb1 = remote(mb.at[2], mb.at[2], pair_s.at[4], pair_r.at[4], partner)

    @pl.when(s == 0)
    def _():
        c_gw.wait_recv()
        mb[0] = mixacc[...]
        mb[1] = dot(pw[...], gw[...], 1, 1)
        c_mb0.start()

    @pl.when(s == 1)
    def _():
        mb[2] = mixacc[...]
        c_mb1.start()

    for j in range(7, 10):
        event(j, True)

    @pl.when(s == 0)
    def _():
        c_mb1.wait_recv()

    @pl.when(s == 1)
    def _():
        c_mb0.wait_recv()

    mt = jnp.concatenate(
        [jnp.concatenate([mb[0], mb[1]], axis=1), jnp.concatenate([jnp.zeros((T, T), F32), mb[2]], axis=1)], axis=0
    )
    mth = mt.astype(BF)
    mt2[0] = mth
    mt2[1] = (mt - mth.astype(F32)).astype(BF)
    m = mt.T
    mh = m.astype(BF)
    m2[0] = mh
    m2[1] = (m - mh.astype(F32)).astype(BF)

    def turn_own(zb, carry):
        xt[zb, :, 0:256] = xs[p1, zb].T
        return carry

    lax.fori_loop(0, 8, turn_own, 0)

    for j in range(10, 14):
        event(j, False)
        k = j - 9
        if k == 4:
            break
        remote(xs.at[(p1 + k) % 4], xr.at[k - 1], xr_s.at[k - 1], xr_r.at[k - 1], first(k)).wait_recv()

        def turn(zb, carry, k=k):
            xt[zb, :, k * 256 : (k + 1) * 256] = xr[k - 1, zb].T
            return carry

        lax.fori_loop(0, 8, turn, 0)
        remote(ds16.at[(p1 + k) % 4], dr16.at[k - 1], dr_s.at[k - 1], dr_r.at[k - 1], first(k)).wait_recv()

    c_psel = remote(psel, prem, pair_s.at[2], pair_r.at[2], partner)
    c_psel.start()

    c_psel.wait_recv()
    sel[...] = ((psel[...] + prem[...]) * (1.0 / math.sqrt(8192.0))).astype(BF)
    bmap = sel[:, 0:T]
    cmap = sel[:, T : 2 * T]
    d_in = dot(mt2[0], cmap) + dot(mt2[1], cmap)
    d_out = dot(m2[0], bmap) + dot(m2[1], bmap)
    sall[0] = jnp.concatenate([d_in, d_out], axis=1).astype(BF)
    for k in range(1, 4):
        remote(sall.at[0], sall.at[k], s_s.at[k - 1], s_r.at[k - 1], first(k)).start()
    c_sg = pltpu.make_async_copy(sall.at[0, pl.ds(pl.multiple_of(s * T, T), T)], sg_hbm, outs.at[0])
    c_sg.start()

    mine = pl.ds(pl.multiple_of(s * T, T), T)
    inter = dot(sel[mine, 0:T], sel[mine, T : 2 * T], 1, 1).astype(BF)
    across = (dot(sel[0:T, 0:T], sel[T : 2 * T, T : 2 * T], 1, 1) * (1 - s).astype(F32)).astype(BF)

    def grads(start, stop):
        def one(j, carry):
            off = pl.ds(pl.multiple_of(j * 128, 128), 128)
            dp = dy[:, off]
            lhs = jnp.concatenate([e_all[2 * j] * inter, e_all[2 * j + 1] * inter], axis=1)
            rhs = jnp.concatenate([jnp.where(low, dp, none), jnp.where(low, none, dp)], axis=0)
            out = dot(lhs, rhs) + ewx[:, off].astype(F32) * dot(across, gw[:, off])
            ig[:, off] = out.astype(BF)
            return carry

        lax.fori_loop(start, stop, one, 0)

    grads(0, 26)

    for k in range(1, 4):
        remote(sall.at[0], sall.at[k], s_s.at[k - 1], s_r.at[k - 1], first(k)).wait_recv()

    scale = 0.5 / math.sqrt(8192.0)

    def weight(zb, carry):
        gf[zb] = dot(xt[zb], sall[...].reshape(1024, 256)) * scale
        return carry

    lax.fori_loop(0, 8, weight, 0)
    drift = dr[pl.ds(pl.multiple_of(p1 * 128, 128), 128), :]
    for k in range(3):
        drift = drift + dr16[k].astype(F32)
    gf[z] = gf[z] - drift
    for q in range(4):
        gs[q] = gf[:, q * 32 : (q + 1) * 32, :].astype(BF)
    for k in range(1, 4):
        remote(gs.at[(p2 + k) % 4], r2.at[k - 1], p_s.at[k - 1], p_r.at[k - 1], second(k)).start()
    grads(26, 48)
    total = gf[:, pl.ds(pl.multiple_of(p2 * 32, 32), 32), :]
    for k in range(1, 4):
        remote(gs.at[(p2 + k) % 4], r2.at[k - 1], p_s.at[k - 1], p_r.at[k - 1], second(k)).wait_recv()
        total = total + r2[k - 1].astype(F32)
    t2[...] = total
    t2b[...] = total.astype(BF)
    for k in range(1, 8):
        remote(t2b.at[(z + k) % 8], r3.at[k - 1], z_s.at[k - 1], z_r.at[k - 1], along(k)).start()
    grads(48, 64)
    c_ig = pltpu.make_async_copy(ig, ig_hbm, outs.at[1])
    c_ig.start()
    part = t2[z]
    for k in range(1, 8):
        remote(t2b.at[(z + k) % 8], r3.at[k - 1], z_s.at[k - 1], z_r.at[k - 1], along(k)).wait_recv()
        part = part + r3[k - 1].astype(F32)
    mine_at = p1 * 4 + p2
    dl[mine_at] = (part * (1.0 / 16.0)).astype(BF)

    def plane(k):
        return remote(
            dl.at[mine_at], dl.at[mine_at], a_s.at[k - 1], a_r.at[k - 1], {"seq": s, "dp": z, "island": (isl + k) % 16}
        )

    def share(k, carry):
        plane(k).start()
        return carry

    lax.fori_loop(1, 16, share, 0)

    def arrived(k, carry):
        other = (isl + 16 - k) % 16
        oy = other // 4
        ox = other % 4
        at = dl.at[(ox + s * (oy - ox)) * 4 + oy + s * (ox - oy)]
        remote(at, at, a_s.at[k - 1], a_r.at[k - 1], partner).wait_recv()
        return carry

    lax.fori_loop(1, 16, arrived, 0)
    c_delta = pltpu.make_async_copy(dl, delta_hbm, outs.at[2])
    c_delta.start()

    def drain(j, carry):
        right(j, z, 0).wait_send()
        left(j, z, 0).wait_send()
        return carry

    lax.fori_loop(0, EVENTS, drain, 0)
    remote(own_x, other_x, pair_s.at[0], pair_r.at[0], partner).wait_send()
    c_psel.wait_send()

    @pl.when(s == 0)
    def _():
        c_mb0.wait_send()

    @pl.when(s == 1)
    def _():
        c_gw.wait_send()
        c_mb1.wait_send()

    for k in range(1, 4):
        remote(xs.at[0], xr.at[k - 1], xr_s.at[k - 1], xr_r.at[k - 1], first(k)).wait_send()
        remote(ds16.at[0], dr16.at[k - 1], dr_s.at[k - 1], dr_r.at[k - 1], first(k)).wait_send()
        remote(sall.at[0], sall.at[k], s_s.at[k - 1], s_r.at[k - 1], first(k)).wait_send()
        remote(gs.at[0], r2.at[k - 1], p_s.at[k - 1], p_r.at[k - 1], second(k)).wait_send()
    for k in range(1, 8):
        remote(t2b.at[0], r3.at[k - 1], z_s.at[k - 1], z_r.at[k - 1], along(k)).wait_send()

    def left_here(k, carry):
        plane(k).wait_send()
        return carry

    lax.fori_loop(1, 16, left_here, 0)
    c_sg.wait()
    c_ig.wait()
    c_delta.wait()


def finish(ig, sg, dl, mo, ow, ig_out, sg_out, mo_out, ow_out, igv, sgv, dlv, mov, owv, nmv, nov, ins, outs):
    loads = [
        pltpu.make_async_copy(dl, dlv, ins.at[0]),
        pltpu.make_async_copy(mo, mov, ins.at[1]),
        pltpu.make_async_copy(ow, owv, ins.at[2]),
        pltpu.make_async_copy(sg, sgv, ins.at[3]),
    ]
    parts = [pl.ds(2048 * c, 2048) for c in range(4)]
    moves = [pltpu.make_async_copy(ig.at[:, p], igv.at[:, p], ins.at[4 + c]) for c, p in enumerate(parts)]
    for c in loads + moves:
        c.start()
    ends = []
    for c, p in enumerate(parts):
        moves[c].wait()
        ends.append(pltpu.make_async_copy(igv.at[:, p], ig_out.at[:, p], outs.at[4 + c]))
        ends[c].start()
    for c in loads:
        c.wait()
    c_sg = pltpu.make_async_copy(sgv, sg_out, outs.at[1])
    c_sg.start()
    delta = dlv[...].reshape(512, 256).astype(F32)
    momentum = 0.9 * mov[...] + delta
    nmv[...] = momentum
    c_mo = pltpu.make_async_copy(nmv, mo_out, outs.at[2])
    c_mo.start()
    nov[...] = owv[...] - 0.7 * (delta + 0.9 * momentum)
    c_ow = pltpu.make_async_copy(nov, ow_out, outs.at[3])
    c_ow.start()
    for c in ends + [c_sg, c_mo, c_ow]:
        c.wait()


def local(layer_input, inner_acts, out_grad, step_sizes, outer_weight, island_drift, momentum):
    anyspec = pl.BlockSpec(memory_space=pl.ANY)
    dma = pltpu.SemaphoreType.DMA
    vm = pltpu.VMEM
    in_grad, sel_grad, delta = pl.pallas_call(
        kernel,
        out_shape=(
            jax.ShapeDtypeStruct((T, 8192), BF),
            jax.ShapeDtypeStruct((T, 256), BF),
            jax.ShapeDtypeStruct((16, 32, 256), BF),
        ),
        in_specs=[pl.BlockSpec(memory_space=pltpu.HBM)] * 6,
        out_specs=(anyspec, anyspec, anyspec),
        scratch_shapes=[
            vm((512, 256), F32),
            vm((512, 256), F32),
            vm((T, HEADS), F32),
            vm((T, 8192), BF),
            vm((T, 8192), BF),
            vm((8, 4, 128, 256), BF),
            vm((4, 8, 256, 128), BF),
            vm((3, 8, 256, 128), BF),
            vm((8, 128, 1024), BF),
            vm((4, 128, 256), BF),
            vm((3, 128, 256), BF),
            vm((T, HEADS), F32),
            vm((HEADS, T), F32),
            vm((T, T), F32),
            vm((T, 2 * T), BF),
            vm((T, 8192), BF),
            vm((T, 8192), BF),
            vm((T, 8192), BF),
            vm((HEADS, T, T), BF),
            vm((T, 8192), BF),
            vm((3, T, T), F32),
            vm((2, 256, 256), BF),
            vm((2, 256, 256), BF),
            vm((256, 256), F32),
            vm((256, 256), F32),
            vm((256, 256), BF),
            vm((4, 256, 256), BF),
            vm((8, 128, 256), F32),
            vm((4, 8, 32, 256), BF),
            vm((3, 8, 32, 256), BF),
            vm((8, 32, 256), F32),
            vm((8, 32, 256), BF),
            vm((7, 32, 256), BF),
            vm((16, 32, 256), BF),
            dma((6,)),
            dma((2, EVENTS)),
            dma((2, EVENTS)),
            dma((5,)),
            dma((5,)),
            dma((3,)), dma((3,)),
            dma((3,)), dma((3,)),
            dma((3,)), dma((3,)),
            dma((3,)), dma((3,)),
            dma((7,)), dma((7,)),
            dma((15,)), dma((15,)),
            dma((3,)),
        ],
        compiler_params=pltpu.CompilerParams(
            collective_id=0, has_side_effects=True, vmem_limit_bytes=VMEM_LIMIT
        ),
    )(
        layer_input[0, 0], inner_acts[0, 0], out_grad[0, 0], step_sizes[0, 0], outer_weight, island_drift[0]
    )
    in_grad, sel_grad, new_momentum, new_outer = pl.pallas_call(
        finish,
        out_shape=(
            jax.ShapeDtypeStruct((T, 8192), BF),
            jax.ShapeDtypeStruct((T, 256), BF),
            jax.ShapeDtypeStruct((512, 256), F32),
            jax.ShapeDtypeStruct((512, 256), F32),
        ),
        in_specs=[anyspec] * 5,
        out_specs=(pl.BlockSpec(memory_space=pltpu.HBM),) * 4,
        scratch_shapes=[
            vm((T, 8192), BF), vm((T, 256), BF), vm((16, 32, 256), BF),
            vm((512, 256), F32), vm((512, 256), F32), vm((512, 256), F32), vm((512, 256), F32),
            dma((8,)), dma((8,)),
        ],
        compiler_params=pltpu.CompilerParams(vmem_limit_bytes=FINISH_LIMIT),
    )(in_grad, sel_grad, delta, momentum, outer_weight)
    return (in_grad[None, None], sel_grad[None, None], new_momentum, new_outer)


def solution(mesh):
    acts = P("island", "dp", "seq", None)
    rows = P(("seq", "dp"), None)
    return jax.shard_map(
        local,
        mesh=mesh,
        in_specs=(acts, acts, acts, acts, rows, P("island", ("seq", "dp"), None), rows),
        out_specs=(acts, acts, rows, rows),
        check_vma=False,
    )
```

```python
import functools
import math

import jax
import jax.numpy as jnp
from jax import lax
from jax.experimental import pallas as pl
from jax.experimental.pallas import tpu as pltpu
from jax.sharding import PartitionSpec as P

MESH = pl.DeviceIdType.MESH
BF = jnp.bfloat16
F32 = jnp.float32
HEADS = 128
T = 128
NZ = 8
NQ = 4
EVENTS = 14
VMEM_LIMIT = 60 * 1024 * 1024
FINISH_LIMIT = 62 * 1024 * 1024


def dot(a, b, ca=1, cb=0):
    return lax.dot_general(a, b, (((ca,), (cb,)), ((), ())), preferred_element_type=F32)


def remote(src, dst, send, recv, device):
    return pltpu.make_async_remote_copy(
        src_ref=src, dst_ref=dst, send_sem=send, recv_sem=recv, device_id=device, device_id_type=MESH
    )


def kernel(
    x_hbm, ia_hbm, dy_hbm, dt_hbm, ow_hbm, dr_hbm,
    ig_hbm, sg_hbm, delta_hbm,
    ow, dr, dt, ia, dy, wg, xs, xr, xt, ds16, dr16,
    lq, lt, mixacc, ew, pw, ewx, gw, e_all, ig, mb, mt2, m2,
    psel, prem, sel, sall, gf, gs, r2, t2, t2b, r3, dl,
    loc, ring_s, ring_r, pair_s, pair_r, xr_s, xr_r, dr_s, dr_r,
    s_s, s_r, p_s, p_r, z_s, z_r, a_s, a_r, outs,
):
    s = lax.axis_index("seq")
    z = lax.axis_index("dp")
    isl = lax.axis_index("island")
    y = isl // 4
    x = isl % 4
    p1 = x + s * (y - x)
    p2 = y + s * (x - y)
    base1 = (1 - s) * 4 * y + s * x
    mul1 = 1 + 3 * s
    base2 = (1 - s) * x + s * 4 * y
    mul2 = 4 - 3 * s

    def first(k):
        return {"seq": s, "dp": z, "island": base1 + mul1 * ((p1 + k) % 4)}

    def second(k):
        return {"seq": s, "dp": z, "island": base2 + mul2 * ((p2 + k) % 4)}

    def along(k):
        return {"seq": s, "dp": (z + k) % 8, "island": isl}

    partner = {"seq": 1 - s, "dp": z, "island": isl}

    barrier = pltpu.get_barrier_semaphore()
    peers = [partner, along(1), along(7)] + [d(k) for d in (first, second) for k in (1, 2, 3)]
    for d in peers:
        pl.semaphore_signal(barrier, inc=1, device_id=d, device_id_type=MESH)

    c_ow = pltpu.make_async_copy(ow_hbm, ow, loc.at[0])
    c_dr = pltpu.make_async_copy(dr_hbm, dr, loc.at[1])
    c_dt = pltpu.make_async_copy(dt_hbm, dt, loc.at[2])
    c_ia = pltpu.make_async_copy(ia_hbm, ia, loc.at[3])
    c_dy = pltpu.make_async_copy(dy_hbm, dy, loc.at[4])
    for c in (c_ow, c_dr, c_dt, c_dy, c_ia):
        c.start()

    mine = pl.ds(pl.multiple_of(s * T, T), T)
    theirs = pl.ds(pl.multiple_of((1 - s) * T, T), T)
    kept = pl.ds(pl.multiple_of(s * 4096, 128), 4096)
    given = pl.ds(pl.multiple_of((1 - s) * 4096, 128), 4096)
    c_x = pltpu.make_async_copy(x_hbm.at[:, kept], xs.at[mine], loc.at[5])
    c_x.start()

    c_ow.wait()
    c_dr.wait()
    wg[z] = (ow[...] + dr[...]).astype(BF).reshape(4, 128, 256)
    pl.semaphore_wait(barrier, len(peers))

    c_xs = remote(x_hbm.at[:, given], xs.at[mine], pair_s.at[0], pair_r.at[0], partner)
    c_xs.start()

    def right(j, zb, q):
        at = wg.at[zb, q]
        return remote(at, at, ring_s.at[0, j], ring_r.at[0, j], along(1))

    def left(j, zb, q):
        at = wg.at[zb, q]
        return remote(at, at, ring_s.at[1, j], ring_r.at[1, j], along(7))

    for j in range(4):
        right(j, z, j).start()
        left(j, z, 3 - j).start()

    for q in range(4):
        ds16[q] = dr[pl.ds(q * 128, 128), :].astype(BF)

    def columns(zb, q):
        return pl.ds(pl.multiple_of(zb * 512 + q * 128, 128), 128)

    def send_xr(k, zb):
        return remote(
            xs.at[:, columns(zb, (p1 + k) % 4)], xr.at[k - 1, zb], xr_s.at[k - 1], xr_r.at[k - 1], first(k)
        )

    def all_xr(k):
        return remote(xr.at[k - 1], xr.at[k - 1], xr_s.at[k - 1], xr_r.at[k - 1], first(k))

    def send_dr(k):
        return remote(ds16.at[(p1 + k) % 4], dr16.at[k - 1], dr_s.at[k - 1], dr_r.at[k - 1], first(k))

    def spread(k):
        def one(zb, carry):
            send_xr(k, zb).start()
            return carry

        lax.fori_loop(0, 8, one, 0)
        send_dr(k).start()

    def event(j, forward):
        k = j // 4 + 1
        qr = j % 4
        ql = 3 - qr
        zr = (z - k + 8) % 8
        zl = (z + k) % 8
        right(j, zr, qr).wait_recv()
        if forward is not None:

            @pl.when(forward)
            def _():
                right(j + 4, zr, qr).start()

        left(j, zl, ql).wait_recv()
        if forward is not None:

            @pl.when(forward)
            def _():
                left(j + 4, zl, ql).start()

    c_dt.wait()
    rows = lax.broadcasted_iota(jnp.int32, (T, T), 0)
    cols = lax.broadcasted_iota(jnp.int32, (T, T), 1)
    tri = (rows >= cols).astype(F32)
    steps = dt[...]
    levels = lax.dot_general(
        tri, steps, (((1,), (0,)), ((), ())), precision=lax.Precision.HIGHEST, preferred_element_type=F32
    )
    finals = levels[T - 1 : T, :]
    logs = jnp.where(steps > 0.0, jnp.log(jnp.where(steps > 0.0, steps, 1.0)), -1e30)
    lq[...] = levels + logs
    lt[...] = levels.T
    first_core = s == 0
    factor = jnp.exp(jnp.where(first_core, (levels - finals) + logs, -levels))
    hi = factor.astype(BF)
    ew[:, 0:T] = hi
    ew[:, T : 2 * T] = (factor - hi.astype(F32)).astype(BF)
    def widen(c, carry):
        wide = 512
        kk = lax.broadcasted_iota(jnp.int32, (2 * T, wide), 0)
        ll = lax.broadcasted_iota(jnp.int32, (2 * T, wide), 1)
        spread = ((kk % T) == c * 8 + ll // 64).astype(F32).astype(BF)
        fac = dot(ew[...], spread)
        off = pl.ds(pl.multiple_of(c * wide, wide), wide)
        ewx[:, off] = fac.astype(BF)

        @pl.when(s == 0)
        def _():
            pw[:, off] = (ia[:, off].astype(F32) * fac).astype(BF)

        @pl.when(s == 1)
        def _():
            gw[:, off] = (dy[:, off].astype(F32) * fac).astype(BF)

        return carry

    c_gw = remote(gw, gw, pair_s.at[1], pair_r.at[1], partner)
    always = s >= 0
    c_x.wait()
    remote(xs.at[theirs], xs.at[theirs], pair_s.at[0], pair_r.at[0], partner).wait_recv()
    spread(1)
    spread(2)
    spread(3)
    event(0, always)
    c_ia.wait()
    c_dy.wait()
    lax.fori_loop(0, 5, widen, 0)
    event(1, always)
    lax.fori_loop(5, 11, widen, 0)
    event(2, always)
    lax.fori_loop(11, 16, widen, 0)

    @pl.when(s == 1)
    def _():
        c_gw.start()

    event(3, always)
    event(4, always)
    event(5, always)

    mixacc[...] = jnp.zeros((T, T), F32)
    low = lax.broadcasted_iota(jnp.int32, (T, T), 1) < 64
    keep = rows <= cols
    none = jnp.zeros((T, T), BF)

    def group(g):
        shifted = pltpu.roll(lq[...], (128 - 8 * g) % 128, 1)
        lrow = lt[pl.ds(pl.multiple_of(8 * g, 8), 8), :]
        mix = mixacc[...]
        for pair in range(4):
            off = pl.ds(pl.multiple_of(g * 512 + pair * 128, 128), 128)
            xp = ia[:, off]
            both = jnp.concatenate([jnp.where(low, xp, none), jnp.where(low, none, xp)], axis=0)
            scores = dot(both, dy[:, off], 1, 1)
            for u in range(2):
                c = 2 * pair + u
                e = jnp.where(keep, jnp.exp(shifted[:, c : c + 1] - lrow[c : c + 1, :]), 0.0)
                mix = mix + e * scores[u * T : (u + 1) * T, :]
                e_all[g * 8 + c] = e.astype(BF)
        mixacc[...] = mix

    def two_parts(za, qa, zb, qb):
        a = jnp.concatenate([xs[:, columns(za, qa)], xs[:, columns(zb, qb)]], axis=1)
        b = jnp.concatenate([wg[za, qa], wg[zb, qb]], axis=0)
        return dot(a, b)

    def add(both, start):
        for c in range(2):
            half = both[:, c * T : (c + 1) * T]
            psel[c] = half if start else psel[c] + half

    def gain(j, carry):
        k = j // 4 + 1
        add(two_parts((z - k + 8) % 8, j % 4, (z + k) % 8, 3 - j % 4), False)
        return carry

    def group_loop(g, carry):
        group(g)
        return carry

    def busy(j, carry):
        event(j, j < 10)
        lax.fori_loop(3 * j - 18, 3 * j - 15, group_loop, 0)
        return gain(j - 6, carry)

    add(two_parts(z, 0, z, 1) + two_parts(z, 2, z, 3), True)
    lax.fori_loop(6, 11, busy, 0)
    event(11, None)
    group(15)

    c_mb0 = remote(mb.at[pl.ds(0, 2)], mb.at[pl.ds(0, 2)], pair_s.at[3], pair_r.at[3], partner)
    c_mb1 = remote(mb.at[2], mb.at[2], pair_s.at[4], pair_r.at[4], partner)

    @pl.when(s == 0)
    def _():
        c_gw.wait_recv()
        mb[0] = mixacc[...]
        mb[1] = dot(pw[...], gw[...], 1, 1)
        c_mb0.start()

    @pl.when(s == 1)
    def _():
        mb[2] = mixacc[...]
        c_mb1.start()

    lax.fori_loop(5, 12, gain, 0)
    event(12, None)
    gain(12, 0)

    def turn_own(zb, carry):
        xt[pl.ds(pl.multiple_of(zb * 128, 128), 128), 0:256] = xs[:, columns(zb, p1)].T
        return carry

    lax.fori_loop(0, 8, turn_own, 0)
    @pl.when(s == 0)
    def _():
        c_mb1.wait_recv()

    @pl.when(s == 1)
    def _():
        c_mb0.wait_recv()

    mt = jnp.concatenate(
        [jnp.concatenate([mb[0], mb[1]], axis=1), jnp.concatenate([jnp.zeros((T, T), F32), mb[2]], axis=1)], axis=0
    )
    mth = mt.astype(BF)
    mt2[0] = mth
    mt2[1] = (mt - mth.astype(F32)).astype(BF)
    m = mt.T
    mh = m.astype(BF)
    m2[0] = mh
    m2[1] = (m - mh.astype(F32)).astype(BF)

    event(13, None)
    gain(13, 0)
    c_psel = remote(psel, prem, pair_s.at[2], pair_r.at[2], partner)
    c_psel.start()

    inv_root = 1.0 / math.sqrt(8192.0)

    scale = 0.5 * inv_root

    place = {1: 1, 3: 2, 2: 3}

    def send_s(k):
        return remote(sall.at[0], sall.at[place[k]], s_s.at[k - 1], s_r.at[k - 1], first(k))

    c_psel.wait_recv()
    bmap = ((psel[0] + prem[0]) * inv_root).astype(BF)
    cmap = ((psel[1] + prem[1]) * inv_root).astype(BF)
    d_in = dot(mt2[0], cmap) + dot(mt2[1], cmap)
    d_out = dot(m2[0], bmap) + dot(m2[1], bmap)
    sall[0] = jnp.concatenate([d_in, d_out], axis=1).astype(BF)
    for k in (2, 1, 3):
        send_s(k).start()
    c_sg = pltpu.make_async_copy(sall.at[0, mine], sg_hbm, outs.at[0])
    c_sg.start()
    sel[:, 0:T] = bmap
    sel[:, T : 2 * T] = cmap

    inter = dot(sel[mine, 0:T], sel[mine, T : 2 * T], 1, 1).astype(BF)
    across = (dot(sel[0:T, 0:T], sel[T : 2 * T, T : 2 * T], 1, 1) * (1 - s).astype(F32)).astype(BF)

    def grads(start, stop):
        def one(j, carry):
            for u in range(4):
                pair = 4 * j + u
                off = pl.ds(pl.multiple_of(pair * 128, 128), 128)
                dp = dy[:, off]
                lhs = jnp.concatenate([e_all[2 * pair] * inter, e_all[2 * pair + 1] * inter], axis=1)
                rhs = jnp.concatenate([jnp.where(low, dp, none), jnp.where(low, none, dp)], axis=0)
                out = dot(lhs, rhs) + ewx[:, off].astype(F32) * dot(across, gw[:, off])
                ig[:, off] = out.astype(BF)
            return carry

        lax.fori_loop(start // 4, stop // 4, one, 0)

    def ig_out(c):
        part = pl.ds(c * 2048, 2048)
        return pltpu.make_async_copy(ig.at[:, part], ig_hbm.at[:, part], outs.at[1 + c])

    def blocks(half):
        return pl.ds(pl.multiple_of(half * 4, 4), 4), pl.ds(pl.multiple_of(half * 512, 512), 512)

    def own_weight(half, carry):
        four, rows_of = blocks(half)
        gf[four] = dot(xt[rows_of, 0:256], sall[0]).reshape(4, 128, 256)
        return carry

    lax.fori_loop(0, 2, own_weight, 0)
    for k in range(1, 4):
        all_xr(k).wait_recv()

        def turn(zb, carry, k=k):
            at = place[k] * 256
            xt[pl.ds(pl.multiple_of(zb * 128, 128), 128), at : at + 256] = xr[k - 1, zb].T
            return carry

        lax.fori_loop(0, 8, turn, 0)
        send_dr(k).wait_recv()
    drift = dr[pl.ds(pl.multiple_of(p1 * 128, 128), 128), :]
    for k in range(3):
        drift = drift + dr16[k].astype(F32)
    gf[z] = gf[z] - drift * (1.0 / scale)
    grads(0, 16)
    ig_out(0).start()

    def send_p(k):
        return remote(gs.at[(p2 + k) % 4], r2.at[k - 1], p_s.at[k - 1], p_r.at[k - 1], second(k))

    send_s(1).wait_recv()
    send_s(3).wait_recv()

    def near_weight(half, carry):
        four, rows_of = blocks(half)
        gf[four] += dot(xt[rows_of, 256:768], sall[1:3].reshape(512, 256)).reshape(4, 128, 256)
        return carry

    lax.fori_loop(0, 2, near_weight, 0)
    send_s(2).wait_recv()

    def far_weight(half, carry):
        four, rows_of = blocks(half)
        g = (gf[four] + dot(xt[rows_of, 768:1024], sall[3]).reshape(4, 128, 256)) * scale
        gf[four] = g
        for q in range(4):
            gs[q, four] = g[:, q * 32 : (q + 1) * 32].astype(BF)
        return carry

    lax.fori_loop(0, 2, far_weight, 0)
    for k in (2, 1, 3):
        send_p(k).start()
    grads(16, 32)
    ig_out(1).start()

    def send_z(k):
        return remote(t2b.at[(z + k) % 8], r3.at[k - 1], z_s.at[k - 1], z_r.at[k - 1], along(k))

    total = gf[:, pl.ds(pl.multiple_of(p2 * 32, 32), 32), :]
    for k in (1, 3, 2):
        send_p(k).wait_recv()
        total = total + r2[k - 1].astype(F32)
    t2[...] = total
    t2b[...] = total.astype(BF)
    for k in (4, 3, 5, 2, 6, 1, 7):
        send_z(k).start()
    grads(32, 48)
    ig_out(2).start()
    mine_at = p1 * 4 + p2

    def plane(k):
        at = dl.at[mine_at]
        device = {"seq": s, "dp": z, "island": (isl + k) % 16}
        return remote(at, at, a_s.at[k - 1], a_r.at[k - 1], device)

    part = t2[z]
    for k in range(1, 8):
        send_z(k).wait_recv()
        part = part + r3[k - 1].astype(F32)
    dl[mine_at] = (part * (1.0 / 16.0)).astype(BF)

    def share(k, carry):
        plane(k).start()
        return carry

    lax.fori_loop(1, 16, share, 0)
    grads(48, 64)
    ig_out(3).start()

    def arrived(k, carry):
        other = (isl + 16 - k) % 16
        oy = other // 4
        ox = other % 4
        at = dl.at[(ox + s * (oy - ox)) * 4 + oy + s * (ox - oy)]
        remote(at, at, a_s.at[k - 1], a_r.at[k - 1], partner).wait_recv()
        return carry

    lax.fori_loop(1, 16, arrived, 0)
    c_delta = pltpu.make_async_copy(dl, delta_hbm, outs.at[5])
    c_delta.start()

    def drain(j, carry):
        right(j, z, 0).wait_send()
        left(j, z, 0).wait_send()
        return carry

    lax.fori_loop(0, EVENTS, drain, 0)
    c_xs.wait_send()
    c_psel.wait_send()

    @pl.when(s == 0)
    def _():
        c_mb0.wait_send()

    @pl.when(s == 1)
    def _():
        c_gw.wait_send()
        c_mb1.wait_send()

    for k in range(1, 4):
        all_xr(k).wait_send()
        send_dr(k).wait_send()
        send_s(k).wait_send()
        send_p(k).wait_send()
    for k in range(1, 8):
        send_z(k).wait_send()

    def left_here(k, carry):
        plane(k).wait_send()
        return carry

    lax.fori_loop(1, 16, left_here, 0)
    c_sg.wait()
    for c in range(4):
        ig_out(c).wait()
    c_delta.wait()


def finish(ig, sg, dl, mo, ow, ig_out, sg_out, mo_out, ow_out, igv, sgv, dlv, mov, owv, nmv, nov, ins, outs):
    loads = [
        pltpu.make_async_copy(dl, dlv, ins.at[0]),
        pltpu.make_async_copy(mo, mov, ins.at[1]),
        pltpu.make_async_copy(ow, owv, ins.at[2]),
        pltpu.make_async_copy(sg, sgv, ins.at[3]),
    ]
    parts = [pl.ds(2048 * c, 2048) for c in range(4)]
    moves = [pltpu.make_async_copy(ig.at[:, p], igv.at[:, p], ins.at[4 + c]) for c, p in enumerate(parts)]
    for c in loads + moves:
        c.start()
    ends = []
    for c, p in enumerate(parts):
        moves[c].wait()
        ends.append(pltpu.make_async_copy(igv.at[:, p], ig_out.at[:, p], outs.at[4 + c]))
        ends[c].start()
    for c in loads:
        c.wait()
    c_sg = pltpu.make_async_copy(sgv, sg_out, outs.at[1])
    c_sg.start()
    delta = dlv[...].reshape(512, 256).astype(F32)
    momentum = 0.9 * mov[...] + delta
    nmv[...] = momentum
    c_mo = pltpu.make_async_copy(nmv, mo_out, outs.at[2])
    c_mo.start()
    nov[...] = owv[...] - 0.7 * (delta + 0.9 * momentum)
    c_ow = pltpu.make_async_copy(nov, ow_out, outs.at[3])
    c_ow.start()
    for c in ends + [c_sg, c_mo, c_ow]:
        c.wait()


def local(layer_input, inner_acts, out_grad, step_sizes, outer_weight, island_drift, momentum):
    anyspec = pl.BlockSpec(memory_space=pl.ANY)
    dma = pltpu.SemaphoreType.DMA
    vm = pltpu.VMEM
    in_grad, sel_grad, delta = pl.pallas_call(
        kernel,
        out_shape=(
            jax.ShapeDtypeStruct((T, 8192), BF),
            jax.ShapeDtypeStruct((T, 256), BF),
            jax.ShapeDtypeStruct((16, 32, 256), BF),
        ),
        in_specs=[pl.BlockSpec(memory_space=pltpu.HBM)] * 6,
        out_specs=(anyspec, anyspec, anyspec),
        scratch_shapes=[
            vm((512, 256), F32),
            vm((512, 256), F32),
            vm((T, HEADS), F32),
            vm((T, 8192), BF),
            vm((T, 8192), BF),
            vm((8, 4, 128, 256), BF),
            vm((256, 4096), BF),
            vm((3, 8, 256, 128), BF),
            vm((1024, 1024), BF),
            vm((4, 128, 256), BF),
            vm((3, 128, 256), BF),
            vm((T, HEADS), F32),
            vm((HEADS, T), F32),
            vm((T, T), F32),
            vm((T, 2 * T), BF),
            vm((T, 8192), BF),
            vm((T, 8192), BF),
            vm((T, 8192), BF),
            vm((HEADS, T, T), BF),
            vm((T, 8192), BF),
            vm((3, T, T), F32),
            vm((2, 256, 256), BF),
            vm((2, 256, 256), BF),
            vm((2, 256, T), F32),
            vm((2, 256, T), F32),
            vm((256, 256), BF),
            vm((4, 256, 256), BF),
            vm((8, 128, 256), F32),
            vm((4, 8, 32, 256), BF),
            vm((3, 8, 32, 256), BF),
            vm((8, 32, 256), F32),
            vm((8, 32, 256), BF),
            vm((7, 32, 256), BF),
            vm((16, 32, 256), BF),
            dma((6,)),
            dma((2, EVENTS)),
            dma((2, EVENTS)),
            dma((5,)),
            dma((5,)),
            dma((3,)), dma((3,)),
            dma((3,)), dma((3,)),
            dma((3,)), dma((3,)),
            dma((3,)), dma((3,)),
            dma((7,)), dma((7,)),
            dma((15,)), dma((15,)),
            dma((6,)),
        ],
        compiler_params=pltpu.CompilerParams(
            collective_id=0, has_side_effects=True, vmem_limit_bytes=VMEM_LIMIT
        ),
    )(
        layer_input[0, 0], inner_acts[0, 0], out_grad[0, 0], step_sizes[0, 0], outer_weight, island_drift[0]
    )
    in_grad, sel_grad, new_momentum, new_outer = pl.pallas_call(
        finish,
        out_shape=(
            jax.ShapeDtypeStruct((T, 8192), BF),
            jax.ShapeDtypeStruct((T, 256), BF),
            jax.ShapeDtypeStruct((512, 256), F32),
            jax.ShapeDtypeStruct((512, 256), F32),
        ),
        in_specs=[anyspec] * 5,
        out_specs=(pl.BlockSpec(memory_space=pltpu.HBM),) * 4,
        scratch_shapes=[
            vm((T, 8192), BF), vm((T, 256), BF), vm((16, 32, 256), BF),
            vm((512, 256), F32), vm((512, 256), F32), vm((512, 256), F32), vm((512, 256), F32),
            dma((8,)), dma((8,)),
        ],
        compiler_params=pltpu.CompilerParams(vmem_limit_bytes=FINISH_LIMIT),
    )(in_grad, sel_grad, delta, momentum, outer_weight)
    return (in_grad[None, None], sel_grad[None, None], new_momentum, new_outer)


def solution(mesh):
    acts = P("island", "dp", "seq", None)
    rows = P(("seq", "dp"), None)
    return jax.shard_map(
        local,
        mesh=mesh,
        in_specs=(acts, acts, acts, acts, rows, P("island", ("seq", "dp"), None), rows),
        out_specs=(acts, acts, rows, rows),
        check_vma=False,
    )
```

```python
import functools
import math

import jax
import jax.numpy as jnp
from jax import lax
from jax.experimental import pallas as pl
from jax.experimental.pallas import tpu as pltpu
from jax.sharding import PartitionSpec as P

MESH = pl.DeviceIdType.MESH
BF = jnp.bfloat16
F32 = jnp.float32
HEADS = 128
T = 128
NZ = 8
NQ = 4
EVENTS = 14
VMEM_LIMIT = 60 * 1024 * 1024
FINISH_LIMIT = 62 * 1024 * 1024


def dot(a, b, ca=1, cb=0):
    return lax.dot_general(a, b, (((ca,), (cb,)), ((), ())), preferred_element_type=F32)


def remote(src, dst, send, recv, device):
    return pltpu.make_async_remote_copy(
        src_ref=src, dst_ref=dst, send_sem=send, recv_sem=recv, device_id=device, device_id_type=MESH
    )


def kernel(
    x_hbm, ia_hbm, dy_hbm, dt_hbm, ow_hbm, dr_hbm,
    ig_hbm, sg_hbm, delta_hbm,
    ow, dr, dt, ia, dy, wg, xs, xr, xt, ds16, dr16,
    lq, lt, mixacc, ew, pw, ewx, gw, e_all, ig, mb, mt2, m2,
    psel, prem, sel, sall, gf, gs, r2, t2, t2b, r3, dl,
    loc, ring_s, ring_r, pair_s, pair_r, xr_s, xr_r, dr_s, dr_r,
    s_s, s_r, p_s, p_r, z_s, z_r, a_s, a_r, outs,
):
    s = lax.axis_index("seq")
    z = lax.axis_index("dp")
    isl = lax.axis_index("island")
    y = isl // 4
    x = isl % 4
    p1 = x + s * (y - x)
    p2 = y + s * (x - y)
    base1 = (1 - s) * 4 * y + s * x
    mul1 = 1 + 3 * s
    base2 = (1 - s) * x + s * 4 * y
    mul2 = 4 - 3 * s

    def first(k):
        return {"seq": s, "dp": z, "island": base1 + mul1 * ((p1 + k) % 4)}

    def second(k):
        return {"seq": s, "dp": z, "island": base2 + mul2 * ((p2 + k) % 4)}

    def along(k):
        return {"seq": s, "dp": (z + k) % 8, "island": isl}

    partner = {"seq": 1 - s, "dp": z, "island": isl}

    c_ow = pltpu.make_async_copy(ow_hbm, ow, loc.at[0])
    c_dr = pltpu.make_async_copy(dr_hbm, dr, loc.at[1])
    c_dt = pltpu.make_async_copy(dt_hbm, dt, loc.at[2])
    c_ia = pltpu.make_async_copy(ia_hbm, ia, loc.at[3])
    c_dy = pltpu.make_async_copy(dy_hbm, dy, loc.at[4])
    for c in (c_ow, c_dr):
        c.start()

    barrier = pltpu.get_barrier_semaphore()
    peers = [partner, along(1), along(7)] + [d(k) for d in (first, second) for k in (1, 2, 3)]
    for d in peers:
        pl.semaphore_signal(barrier, inc=1, device_id=d, device_id_type=MESH)

    for c in (c_dt, c_dy, c_ia):
        c.start()

    mine = pl.ds(pl.multiple_of(s * T, T), T)
    theirs = pl.ds(pl.multiple_of((1 - s) * T, T), T)
    kept = pl.ds(pl.multiple_of(s * 4096, 128), 4096)
    given = pl.ds(pl.multiple_of((1 - s) * 4096, 128), 4096)
    c_x = pltpu.make_async_copy(x_hbm.at[:, kept], xs.at[mine], loc.at[5])
    c_x.start()

    c_ow.wait()
    c_dr.wait()
    wg[z] = (ow[...] + dr[...]).astype(BF).reshape(4, 128, 256)
    pl.semaphore_wait(barrier, len(peers))

    c_xs = remote(x_hbm.at[:, given], xs.at[mine], pair_s.at[0], pair_r.at[0], partner)
    c_xs.start()

    def right(j, zb, q):
        at = wg.at[zb, q]
        return remote(at, at, ring_s.at[0, j], ring_r.at[0, j], along(1))

    def left(j, zb, q):
        at = wg.at[zb, q]
        return remote(at, at, ring_s.at[1, j], ring_r.at[1, j], along(7))

    for j in range(4):
        right(j, z, j).start()
        left(j, z, 3 - j).start()

    for q in range(4):
        ds16[q] = dr[pl.ds(q * 128, 128), :].astype(BF)

    def columns(zb, q):
        return pl.ds(pl.multiple_of(zb * 512 + q * 128, 128), 128)

    def send_xr(k, zb):
        return remote(
            xs.at[:, columns(zb, (p1 + k) % 4)], xr.at[k - 1, zb], xr_s.at[k - 1], xr_r.at[k - 1], first(k)
        )

    def all_xr(k):
        return remote(xr.at[k - 1], xr.at[k - 1], xr_s.at[k - 1], xr_r.at[k - 1], first(k))

    def send_dr(k):
        return remote(ds16.at[(p1 + k) % 4], dr16.at[k - 1], dr_s.at[k - 1], dr_r.at[k - 1], first(k))

    def spread(k):
        def one(zb, carry):
            send_xr(k, zb).start()
            return carry

        lax.fori_loop(0, 8, one, 0)
        send_dr(k).start()

    def event(j, forward):
        k = j // 4 + 1
        qr = j % 4
        ql = 3 - qr
        zr = (z - k + 8) % 8
        zl = (z + k) % 8
        right(j, zr, qr).wait_recv()
        if forward is not None:

            @pl.when(forward)
            def _():
                right(j + 4, zr, qr).start()

        left(j, zl, ql).wait_recv()
        if forward is not None:

            @pl.when(forward)
            def _():
                left(j + 4, zl, ql).start()

    c_dt.wait()
    rows = lax.broadcasted_iota(jnp.int32, (T, T), 0)
    cols = lax.broadcasted_iota(jnp.int32, (T, T), 1)
    tri = (rows >= cols).astype(F32)
    steps = dt[...]
    levels = lax.dot_general(
        tri, steps, (((1,), (0,)), ((), ())), precision=lax.Precision.HIGHEST, preferred_element_type=F32
    )
    finals = levels[T - 1 : T, :]
    logs = jnp.where(steps > 0.0, jnp.log(jnp.where(steps > 0.0, steps, 1.0)), -1e30)
    lq[...] = levels + logs
    lt[...] = levels.T
    first_core = s == 0
    factor = jnp.exp(jnp.where(first_core, (levels - finals) + logs, -levels))
    hi = factor.astype(BF)
    ew[:, 0:T] = hi
    ew[:, T : 2 * T] = (factor - hi.astype(F32)).astype(BF)
    def widen(c, carry):
        wide = 512
        kk = lax.broadcasted_iota(jnp.int32, (2 * T, wide), 0)
        ll = lax.broadcasted_iota(jnp.int32, (2 * T, wide), 1)
        spread = ((kk % T) == c * 8 + ll // 64).astype(F32).astype(BF)
        fac = dot(ew[...], spread)
        off = pl.ds(pl.multiple_of(c * wide, wide), wide)
        ewx[:, off] = fac.astype(BF)

        @pl.when(s == 0)
        def _():
            pw[:, off] = (ia[:, off].astype(F32) * fac).astype(BF)

        @pl.when(s == 1)
        def _():
            gw[:, off] = (dy[:, off].astype(F32) * fac).astype(BF)

        return carry

    c_gw = remote(gw, gw, pair_s.at[1], pair_r.at[1], partner)
    always = s >= 0
    c_x.wait()
    remote(xs.at[theirs], xs.at[theirs], pair_s.at[0], pair_r.at[0], partner).wait_recv()
    spread(1)
    spread(2)
    spread(3)
    event(0, always)
    c_ia.wait()
    c_dy.wait()
    lax.fori_loop(0, 5, widen, 0)
    event(1, always)
    lax.fori_loop(5, 11, widen, 0)
    event(2, always)
    lax.fori_loop(11, 16, widen, 0)

    @pl.when(s == 1)
    def _():
        c_gw.start()

    event(3, always)
    event(4, always)
    event(5, always)

    mixacc[...] = jnp.zeros((T, T), F32)
    low = lax.broadcasted_iota(jnp.int32, (T, T), 1) < 64
    keep = rows <= cols
    none = jnp.zeros((T, T), BF)

    def group(g):
        shifted = pltpu.roll(lq[...], (128 - 8 * g) % 128, 1)
        lrow = lt[pl.ds(pl.multiple_of(8 * g, 8), 8), :]
        mix = mixacc[...]
        for pair in range(4):
            off = pl.ds(pl.multiple_of(g * 512 + pair * 128, 128), 128)
            xp = ia[:, off]
            both = jnp.concatenate([jnp.where(low, xp, none), jnp.where(low, none, xp)], axis=0)
            scores = dot(both, dy[:, off], 1, 1)
            for u in range(2):
                c = 2 * pair + u
                e = jnp.where(keep, jnp.exp(shifted[:, c : c + 1] - lrow[c : c + 1, :]), 0.0)
                mix = mix + e * scores[u * T : (u + 1) * T, :]
                e_all[g * 8 + c] = e.astype(BF)
        mixacc[...] = mix

    def two_parts(za, qa, zb, qb):
        a = jnp.concatenate([xs[:, columns(za, qa)], xs[:, columns(zb, qb)]], axis=1)
        b = jnp.concatenate([wg[za, qa], wg[zb, qb]], axis=0)
        return dot(a, b)

    def add(both, start):
        for c in range(2):
            half = both[:, c * T : (c + 1) * T]
            psel[c] = half if start else psel[c] + half

    def gain(j, carry):
        k = j // 4 + 1
        add(two_parts((z - k + 8) % 8, j % 4, (z + k) % 8, 3 - j % 4), False)
        return carry

    def group_loop(g, carry):
        group(g)
        return carry

    def busy(j, carry):
        event(j, j < 10)
        lax.fori_loop(3 * j - 18, 3 * j - 15, group_loop, 0)
        gain(2 * j - 12, carry)
        return gain(2 * j - 11, carry)

    add(two_parts(z, 0, z, 1) + two_parts(z, 2, z, 3), True)
    lax.fori_loop(6, 11, busy, 0)
    group(15)

    c_mb0 = remote(mb.at[pl.ds(0, 2)], mb.at[pl.ds(0, 2)], pair_s.at[3], pair_r.at[3], partner)
    c_mb1 = remote(mb.at[2], mb.at[2], pair_s.at[4], pair_r.at[4], partner)

    @pl.when(s == 0)
    def _():
        c_gw.wait_recv()
        mb[0] = mixacc[...]
        mb[1] = dot(pw[...], gw[...], 1, 1)
        c_mb0.start()

    @pl.when(s == 1)
    def _():
        mb[2] = mixacc[...]
        c_mb1.start()

    event(11, None)
    lax.fori_loop(10, 12, gain, 0)
    event(12, None)
    gain(12, 0)

    def turn_own(zb, carry):
        xt[pl.ds(pl.multiple_of(zb * 128, 128), 128), 0:256] = xs[:, columns(zb, p1)].T
        return carry

    @pl.when(s == 0)
    def _():
        c_mb1.wait_recv()

    @pl.when(s == 1)
    def _():
        c_mb0.wait_recv()

    mt = jnp.concatenate(
        [jnp.concatenate([mb[0], mb[1]], axis=1), jnp.concatenate([jnp.zeros((T, T), F32), mb[2]], axis=1)], axis=0
    )
    mth = mt.astype(BF)
    mt2[0] = mth
    mt2[1] = (mt - mth.astype(F32)).astype(BF)
    m = mt.T
    mh = m.astype(BF)
    m2[0] = mh
    m2[1] = (m - mh.astype(F32)).astype(BF)

    event(13, None)
    gain(13, 0)
    c_psel = remote(psel, prem, pair_s.at[2], pair_r.at[2], partner)
    c_psel.start()
    lax.fori_loop(0, 8, turn_own, 0)

    inv_root = 1.0 / math.sqrt(8192.0)

    scale = 0.5 * inv_root

    place = {1: 1, 3: 2, 2: 3}

    def send_s(k):
        return remote(sall.at[0], sall.at[place[k]], s_s.at[k - 1], s_r.at[k - 1], first(k))

    c_psel.wait_recv()
    bmap = ((psel[0] + prem[0]) * inv_root).astype(BF)
    cmap = ((psel[1] + prem[1]) * inv_root).astype(BF)
    d_in = dot(mt2[0], cmap) + dot(mt2[1], cmap)
    d_out = dot(m2[0], bmap) + dot(m2[1], bmap)
    sall[0] = jnp.concatenate([d_in, d_out], axis=1).astype(BF)
    for k in (2, 1, 3):
        send_s(k).start()
    c_sg = pltpu.make_async_copy(sall.at[0, mine], sg_hbm, outs.at[0])
    c_sg.start()
    sel[:, 0:T] = bmap
    sel[:, T : 2 * T] = cmap

    inter = dot(sel[mine, 0:T], sel[mine, T : 2 * T], 1, 1).astype(BF)
    across = (dot(sel[0:T, 0:T], sel[T : 2 * T, T : 2 * T], 1, 1) * (1 - s).astype(F32)).astype(BF)

    def grads(start, stop):
        def one(j, carry):
            for u in range(4):
                pair = 4 * j + u
                off = pl.ds(pl.multiple_of(pair * 128, 128), 128)
                dp = dy[:, off]
                lhs = jnp.concatenate([e_all[2 * pair] * inter, e_all[2 * pair + 1] * inter], axis=1)
                rhs = jnp.concatenate([jnp.where(low, dp, none), jnp.where(low, none, dp)], axis=0)
                out = dot(lhs, rhs) + ewx[:, off].astype(F32) * dot(across, gw[:, off])
                ig[:, off] = out.astype(BF)
            return carry

        lax.fori_loop(start // 4, stop // 4, one, 0)

    def ig_out(c):
        part = pl.ds(c * 2048, 2048)
        return pltpu.make_async_copy(ig.at[:, part], ig_hbm.at[:, part], outs.at[1 + c])

    def blocks(half):
        return pl.ds(pl.multiple_of(half * 4, 4), 4), pl.ds(pl.multiple_of(half * 512, 512), 512)

    def own_weight(half, carry):
        four, rows_of = blocks(half)
        gf[four] = dot(xt[rows_of, 0:256], sall[0]).reshape(4, 128, 256)
        return carry

    lax.fori_loop(0, 2, own_weight, 0)
    for k in range(1, 4):
        all_xr(k).wait_recv()

        def turn(zb, carry, k=k):
            at = place[k] * 256
            xt[pl.ds(pl.multiple_of(zb * 128, 128), 128), at : at + 256] = xr[k - 1, zb].T
            return carry

        lax.fori_loop(0, 8, turn, 0)
        send_dr(k).wait_recv()
    drift = dr[pl.ds(pl.multiple_of(p1 * 128, 128), 128), :]
    for k in range(3):
        drift = drift + dr16[k].astype(F32)
    gf[z] = gf[z] - drift * (1.0 / scale)
    grads(0, 16)
    ig_out(0).start()

    def send_p(k):
        return remote(gs.at[(p2 + k) % 4], r2.at[k - 1], p_s.at[k - 1], p_r.at[k - 1], second(k))

    send_s(1).wait_recv()
    send_s(3).wait_recv()

    def near_weight(half, carry):
        four, rows_of = blocks(half)
        gf[four] += dot(xt[rows_of, 256:768], sall[1:3].reshape(512, 256)).reshape(4, 128, 256)
        return carry

    lax.fori_loop(0, 2, near_weight, 0)
    send_s(2).wait_recv()

    def far_weight(half, carry):
        four, rows_of = blocks(half)
        g = (gf[four] + dot(xt[rows_of, 768:1024], sall[3]).reshape(4, 128, 256)) * scale
        gf[four] = g
        for q in range(4):
            gs[q, four] = g[:, q * 32 : (q + 1) * 32].astype(BF)
        return carry

    lax.fori_loop(0, 2, far_weight, 0)
    for k in (2, 1, 3):
        send_p(k).start()
    grads(16, 32)
    ig_out(1).start()

    def send_z(k):
        return remote(t2b.at[(z + k) % 8], r3.at[k - 1], z_s.at[k - 1], z_r.at[k - 1], along(k))

    total = gf[:, pl.ds(pl.multiple_of(p2 * 32, 32), 32), :]
    for k in (1, 3, 2):
        send_p(k).wait_recv()
        total = total + r2[k - 1].astype(F32)
    t2[...] = total
    t2b[...] = total.astype(BF)
    for k in (4, 3, 5, 2, 6, 1, 7):
        send_z(k).start()
    grads(32, 48)
    ig_out(2).start()
    mine_at = p1 * 4 + p2

    def plane(k):
        at = dl.at[mine_at]
        device = {"seq": s, "dp": z, "island": (isl + k) % 16}
        return remote(at, at, a_s.at[k - 1], a_r.at[k - 1], device)

    part = t2[z]
    for k in range(1, 8):
        send_z(k).wait_recv()
        part = part + r3[k - 1].astype(F32)
    dl[mine_at] = (part * (1.0 / 16.0)).astype(BF)

    def share(k, carry):
        plane(k).start()
        return carry

    lax.fori_loop(1, 16, share, 0)
    grads(48, 64)
    ig_out(3).start()

    def arrived(k, carry):
        other = (isl + 16 - k) % 16
        oy = other // 4
        ox = other % 4
        at = dl.at[(ox + s * (oy - ox)) * 4 + oy + s * (ox - oy)]
        remote(at, at, a_s.at[k - 1], a_r.at[k - 1], partner).wait_recv()
        return carry

    lax.fori_loop(1, 16, arrived, 0)
    c_delta = pltpu.make_async_copy(dl, delta_hbm, outs.at[5])
    c_delta.start()

    def drain(j, carry):
        right(j, z, 0).wait_send()
        left(j, z, 0).wait_send()
        return carry

    lax.fori_loop(0, EVENTS, drain, 0)
    c_xs.wait_send()
    c_psel.wait_send()

    @pl.when(s == 0)
    def _():
        c_mb0.wait_send()

    @pl.when(s == 1)
    def _():
        c_gw.wait_send()
        c_mb1.wait_send()

    for k in range(1, 4):
        all_xr(k).wait_send()
        send_dr(k).wait_send()
        send_s(k).wait_send()
        send_p(k).wait_send()
    for k in range(1, 8):
        send_z(k).wait_send()

    def left_here(k, carry):
        plane(k).wait_send()
        return carry

    lax.fori_loop(1, 16, left_here, 0)
    c_sg.wait()
    for c in range(4):
        ig_out(c).wait()
    c_delta.wait()


def finish(ig, sg, dl, mo, ow, ig_out, sg_out, mo_out, ow_out, igv, sgv, dlv, mov, owv, nmv, nov, ins, outs):
    loads = [
        pltpu.make_async_copy(dl, dlv, ins.at[0]),
        pltpu.make_async_copy(mo, mov, ins.at[1]),
        pltpu.make_async_copy(ow, owv, ins.at[2]),
        pltpu.make_async_copy(sg, sgv, ins.at[3]),
    ]
    parts = [pl.ds(32 * c, 32) for c in range(4)]
    moves = [pltpu.make_async_copy(ig.at[p], igv.at[p], ins.at[4 + c]) for c, p in enumerate(parts)]
    for c in loads + moves:
        c.start()
    ends = []
    for c, p in enumerate(parts):
        moves[c].wait()
        ends.append(pltpu.make_async_copy(igv.at[p], ig_out.at[p], outs.at[4 + c]))
        ends[c].start()
    for c in loads:
        c.wait()
    c_sg = pltpu.make_async_copy(sgv, sg_out, outs.at[1])
    c_sg.start()
    delta = dlv[...].reshape(512, 256).astype(F32)
    momentum = 0.9 * mov[...] + delta
    nmv[...] = momentum
    c_mo = pltpu.make_async_copy(nmv, mo_out, outs.at[2])
    c_mo.start()
    nov[...] = owv[...] - 0.7 * (delta + 0.9 * momentum)
    c_ow = pltpu.make_async_copy(nov, ow_out, outs.at[3])
    c_ow.start()
    for c in ends + [c_sg, c_mo, c_ow]:
        c.wait()


def local(layer_input, inner_acts, out_grad, step_sizes, outer_weight, island_drift, momentum):
    anyspec = pl.BlockSpec(memory_space=pl.ANY)
    dma = pltpu.SemaphoreType.DMA
    vm = pltpu.VMEM
    in_grad, sel_grad, delta = pl.pallas_call(
        kernel,
        out_shape=(
            jax.ShapeDtypeStruct((T, 8192), BF),
            jax.ShapeDtypeStruct((T, 256), BF),
            jax.ShapeDtypeStruct((16, 32, 256), BF),
        ),
        in_specs=[pl.BlockSpec(memory_space=pltpu.HBM)] * 6,
        out_specs=(anyspec, anyspec, anyspec),
        scratch_shapes=[
            vm((512, 256), F32),
            vm((512, 256), F32),
            vm((T, HEADS), F32),
            vm((T, 8192), BF),
            vm((T, 8192), BF),
            vm((8, 4, 128, 256), BF),
            vm((256, 4096), BF),
            vm((3, 8, 256, 128), BF),
            vm((1024, 1024), BF),
            vm((4, 128, 256), BF),
            vm((3, 128, 256), BF),
            vm((T, HEADS), F32),
            vm((HEADS, T), F32),
            vm((T, T), F32),
            vm((T, 2 * T), BF),
            vm((T, 8192), BF),
            vm((T, 8192), BF),
            vm((T, 8192), BF),
            vm((HEADS, T, T), BF),
            vm((T, 8192), BF),
            vm((3, T, T), F32),
            vm((2, 256, 256), BF),
            vm((2, 256, 256), BF),
            vm((2, 256, T), F32),
            vm((2, 256, T), F32),
            vm((256, 256), BF),
            vm((4, 256, 256), BF),
            vm((8, 128, 256), F32),
            vm((4, 8, 32, 256), BF),
            vm((3, 8, 32, 256), BF),
            vm((8, 32, 256), F32),
            vm((8, 32, 256), BF),
            vm((7, 32, 256), BF),
            vm((16, 32, 256), BF),
            dma((6,)),
            dma((2, EVENTS)),
            dma((2, EVENTS)),
            dma((5,)),
            dma((5,)),
            dma((3,)), dma((3,)),
            dma((3,)), dma((3,)),
            dma((3,)), dma((3,)),
            dma((3,)), dma((3,)),
            dma((7,)), dma((7,)),
            dma((15,)), dma((15,)),
            dma((6,)),
        ],
        compiler_params=pltpu.CompilerParams(
            collective_id=0, has_side_effects=True, vmem_limit_bytes=VMEM_LIMIT
        ),
    )(
        layer_input[0, 0], inner_acts[0, 0], out_grad[0, 0], step_sizes[0, 0], outer_weight, island_drift[0]
    )
    in_grad, sel_grad, new_momentum, new_outer = pl.pallas_call(
        finish,
        out_shape=(
            jax.ShapeDtypeStruct((T, 8192), BF),
            jax.ShapeDtypeStruct((T, 256), BF),
            jax.ShapeDtypeStruct((512, 256), F32),
            jax.ShapeDtypeStruct((512, 256), F32),
        ),
        in_specs=[anyspec] * 5,
        out_specs=(pl.BlockSpec(memory_space=pltpu.HBM),) * 4,
        scratch_shapes=[
            vm((T, 8192), BF), vm((T, 256), BF), vm((16, 32, 256), BF),
            vm((512, 256), F32), vm((512, 256), F32), vm((512, 256), F32), vm((512, 256), F32),
            dma((8,)), dma((8,)),
        ],
        compiler_params=pltpu.CompilerParams(vmem_limit_bytes=FINISH_LIMIT),
    )(in_grad, sel_grad, delta, momentum, outer_weight)
    return (in_grad[None, None], sel_grad[None, None], new_momentum, new_outer)


def solution(mesh):
    acts = P("island", "dp", "seq", None)
    rows = P(("seq", "dp"), None)
    return jax.shard_map(
        local,
        mesh=mesh,
        in_specs=(acts, acts, acts, acts, rows, P("island", ("seq", "dp"), None), rows),
        out_specs=(acts, acts, rows, rows),
        check_vma=False,
    )
```

```python
import functools
import math

import jax
import jax.numpy as jnp
from jax import lax
from jax.experimental import pallas as pl
from jax.experimental.pallas import tpu as pltpu
from jax.sharding import PartitionSpec as P

MESH = pl.DeviceIdType.MESH
BF = jnp.bfloat16
F32 = jnp.float32
HEADS = 128
T = 128
NZ = 8
NQ = 4
EVENTS = 14
VMEM_LIMIT = 60 * 1024 * 1024
FINISH_LIMIT = 62 * 1024 * 1024


def dot(a, b, ca=1, cb=0):
    return lax.dot_general(a, b, (((ca,), (cb,)), ((), ())), preferred_element_type=F32)


def remote(src, dst, send, recv, device):
    return pltpu.make_async_remote_copy(
        src_ref=src, dst_ref=dst, send_sem=send, recv_sem=recv, device_id=device, device_id_type=MESH
    )


def kernel(
    x_hbm, ia_hbm, dy_hbm, dt_hbm, ow_hbm, dr_hbm,
    ig_hbm, sg_hbm, delta_hbm,
    ow, dr, dt, ia, dy, wg, xs, xr, xt, ds16, dr16,
    lq, lt, mixacc, ew, pw, ewx, gw, e_all, ig, mb, mt2, m2,
    psel, prem, sel, sall, gf, gs, r2, t2, t2b, r3, dl,
    loc, ring_s, ring_r, pair_s, pair_r, xr_s, xr_r, dr_s, dr_r,
    s_s, s_r, p_s, p_r, z_s, z_r, a_s, a_r, outs,
):
    s = lax.axis_index("seq")
    z = lax.axis_index("dp")
    isl = lax.axis_index("island")
    y = isl // 4
    x = isl % 4
    p1 = x + s * (y - x)
    p2 = y + s * (x - y)
    base1 = (1 - s) * 4 * y + s * x
    mul1 = 1 + 3 * s
    base2 = (1 - s) * x + s * 4 * y
    mul2 = 4 - 3 * s

    def first(k):
        return {"seq": s, "dp": z, "island": base1 + mul1 * ((p1 + k) % 4)}

    def second(k):
        return {"seq": s, "dp": z, "island": base2 + mul2 * ((p2 + k) % 4)}

    def along(k):
        return {"seq": s, "dp": (z + k) % 8, "island": isl}

    partner = {"seq": 1 - s, "dp": z, "island": isl}

    c_ow = pltpu.make_async_copy(ow_hbm, ow, loc.at[0])
    c_dr = pltpu.make_async_copy(dr_hbm, dr, loc.at[1])
    c_dt = pltpu.make_async_copy(dt_hbm, dt, loc.at[2])
    c_ia = pltpu.make_async_copy(ia_hbm, ia, loc.at[3])
    c_dy = pltpu.make_async_copy(dy_hbm, dy, loc.at[4])
    for c in (c_ow, c_dr):
        c.start()

    barrier = pltpu.get_barrier_semaphore()
    peers = [partner, along(1), along(7)] + [d(k) for d in (first, second) for k in (1, 2, 3)]
    for d in peers:
        pl.semaphore_signal(barrier, inc=1, device_id=d, device_id_type=MESH)

    for c in (c_dt, c_dy, c_ia):
        c.start()

    mine = pl.ds(pl.multiple_of(s * T, T), T)
    theirs = pl.ds(pl.multiple_of((1 - s) * T, T), T)
    kept = pl.ds(pl.multiple_of(s * 4096, 128), 4096)
    given = pl.ds(pl.multiple_of((1 - s) * 4096, 128), 4096)
    c_x = pltpu.make_async_copy(x_hbm.at[:, kept], xs.at[mine], loc.at[5])
    c_x.start()

    c_ow.wait()
    c_dr.wait()
    wg[z] = (ow[...] + dr[...]).astype(BF).reshape(4, 128, 256)
    pl.semaphore_wait(barrier, len(peers))

    c_xs = remote(x_hbm.at[:, given], xs.at[mine], pair_s.at[0], pair_r.at[0], partner)
    c_xs.start()

    def right(j, zb, q):
        at = wg.at[zb, q]
        return remote(at, at, ring_s.at[0, j], ring_r.at[0, j], along(1))

    def left(j, zb, q):
        at = wg.at[zb, q]
        return remote(at, at, ring_s.at[1, j], ring_r.at[1, j], along(7))

    for j in range(4):
        right(j, z, j).start()
        left(j, z, 3 - j).start()

    for q in range(4):
        ds16[q] = dr[pl.ds(q * 128, 128), :].astype(BF)

    def columns(zb, q):
        return pl.ds(pl.multiple_of(zb * 512 + q * 128, 128), 128)

    def send_xr(k, zb):
        return remote(
            xs.at[:, columns(zb, (p1 + k) % 4)], xr.at[k - 1, zb], xr_s.at[k - 1], xr_r.at[k - 1], first(k)
        )

    def all_xr(k):
        return remote(xr.at[k - 1], xr.at[k - 1], xr_s.at[k - 1], xr_r.at[k - 1], first(k))

    def send_dr(k):
        return remote(ds16.at[(p1 + k) % 4], dr16.at[k - 1], dr_s.at[k - 1], dr_r.at[k - 1], first(k))

    def spread(k):
        def one(zb, carry):
            send_xr(k, zb).start()
            return carry

        lax.fori_loop(0, 8, one, 0)
        send_dr(k).start()

    def event(j, forward):
        k = j // 4 + 1
        qr = j % 4
        ql = 3 - qr
        zr = (z - k + 8) % 8
        zl = (z + k) % 8
        right(j, zr, qr).wait_recv()
        if forward is not None:

            @pl.when(forward)
            def _():
                right(j + 4, zr, qr).start()

        left(j, zl, ql).wait_recv()
        if forward is not None:

            @pl.when(forward)
            def _():
                left(j + 4, zl, ql).start()

    c_dt.wait()
    rows = lax.broadcasted_iota(jnp.int32, (T, T), 0)
    cols = lax.broadcasted_iota(jnp.int32, (T, T), 1)
    tri = (rows >= cols).astype(F32)
    steps = dt[...]
    levels = lax.dot_general(
        tri, steps, (((1,), (0,)), ((), ())), precision=lax.Precision.HIGHEST, preferred_element_type=F32
    )
    finals = levels[T - 1 : T, :]
    logs = jnp.where(steps > 0.0, jnp.log(jnp.where(steps > 0.0, steps, 1.0)), -1e30)
    lq[...] = levels + logs
    lt[...] = levels.T
    first_core = s == 0
    factor = jnp.exp(jnp.where(first_core, (levels - finals) + logs, -levels))
    hi = factor.astype(BF)
    ew[:, 0:T] = hi
    ew[:, T : 2 * T] = (factor - hi.astype(F32)).astype(BF)
    def widen(c, carry):
        wide = 512
        kk = lax.broadcasted_iota(jnp.int32, (2 * T, wide), 0)
        ll = lax.broadcasted_iota(jnp.int32, (2 * T, wide), 1)
        spread = ((kk % T) == c * 8 + ll // 64).astype(F32).astype(BF)
        fac = dot(ew[...], spread)
        off = pl.ds(pl.multiple_of(c * wide, wide), wide)
        ewx[:, off] = fac.astype(BF)

        @pl.when(s == 0)
        def _():
            pw[:, off] = (ia[:, off].astype(F32) * fac).astype(BF)

        @pl.when(s == 1)
        def _():
            gw[:, off] = (dy[:, off].astype(F32) * fac).astype(BF)

        return carry

    c_gw = remote(gw, gw, pair_s.at[1], pair_r.at[1], partner)
    always = s >= 0
    c_x.wait()
    remote(xs.at[theirs], xs.at[theirs], pair_s.at[0], pair_r.at[0], partner).wait_recv()
    spread(1)
    spread(2)
    spread(3)
    event(0, always)
    c_ia.wait()
    c_dy.wait()
    lax.fori_loop(0, 5, widen, 0)
    event(1, always)
    lax.fori_loop(5, 11, widen, 0)
    event(2, always)
    lax.fori_loop(11, 16, widen, 0)

    @pl.when(s == 1)
    def _():
        c_gw.start()

    event(3, always)
    event(4, always)
    event(5, always)

    mixacc[...] = jnp.zeros((T, T), F32)
    low = lax.broadcasted_iota(jnp.int32, (T, T), 1) < 64
    keep = rows <= cols
    none = jnp.zeros((T, T), BF)

    def group(g):
        shifted = pltpu.roll(lq[...], (128 - 8 * g) % 128, 1)
        lrow = lt[pl.ds(pl.multiple_of(8 * g, 8), 8), :]
        mix = mixacc[...]
        for pair in range(4):
            off = pl.ds(pl.multiple_of(g * 512 + pair * 128, 128), 128)
            xp = ia[:, off]
            both = jnp.concatenate([jnp.where(low, xp, none), jnp.where(low, none, xp)], axis=0)
            scores = dot(both, dy[:, off], 1, 1)
            for u in range(2):
                c = 2 * pair + u
                e = jnp.where(keep, jnp.exp(shifted[:, c : c + 1] - lrow[c : c + 1, :]), 0.0)
                mix = mix + e * scores[u * T : (u + 1) * T, :]
                e_all[g * 8 + c] = e.astype(BF)
        mixacc[...] = mix

    def two_parts(za, qa, zb, qb):
        a = jnp.concatenate([xs[:, columns(za, qa)], xs[:, columns(zb, qb)]], axis=1)
        b = jnp.concatenate([wg[za, qa], wg[zb, qb]], axis=0)
        return dot(a, b)

    def add(both, start):
        for c in range(2):
            half = both[:, c * T : (c + 1) * T]
            psel[c] = half if start else psel[c] + half

    def gain(j, carry):
        k = j // 4 + 1
        add(two_parts((z - k + 8) % 8, j % 4, (z + k) % 8, 3 - j % 4), False)
        return carry

    def group_loop(g, carry):
        group(g)
        return carry

    def busy(j, carry):
        event(j, j < 10)
        lax.fori_loop(3 * j - 18, 3 * j - 15, group_loop, 0)
        gain(2 * j - 12, carry)
        return gain(2 * j - 11, carry)

    add(two_parts(z, 0, z, 1) + two_parts(z, 2, z, 3), True)
    lax.fori_loop(6, 11, busy, 0)
    group(15)

    c_mb0 = remote(mb.at[pl.ds(0, 2)], mb.at[pl.ds(0, 2)], pair_s.at[3], pair_r.at[3], partner)
    c_mb1 = remote(mb.at[2], mb.at[2], pair_s.at[4], pair_r.at[4], partner)

    @pl.when(s == 0)
    def _():
        c_gw.wait_recv()
        mb[0] = mixacc[...]
        mb[1] = dot(pw[...], gw[...], 1, 1)
        c_mb0.start()

    @pl.when(s == 1)
    def _():
        mb[2] = mixacc[...]
        c_mb1.start()

    event(11, None)
    lax.fori_loop(10, 12, gain, 0)
    event(12, None)
    gain(12, 0)

    def turn_own(zb, carry):
        xt[pl.ds(pl.multiple_of(zb * 128, 128), 128), 0:256] = xs[:, columns(zb, p1)].T
        return carry

    @pl.when(s == 0)
    def _():
        c_mb1.wait_recv()

    @pl.when(s == 1)
    def _():
        c_mb0.wait_recv()

    mt = jnp.concatenate(
        [jnp.concatenate([mb[0], mb[1]], axis=1), jnp.concatenate([jnp.zeros((T, T), F32), mb[2]], axis=1)], axis=0
    )
    mth = mt.astype(BF)
    mt2[0] = mth
    mt2[1] = (mt - mth.astype(F32)).astype(BF)
    m = mt.T
    mh = m.astype(BF)
    m2[0] = mh
    m2[1] = (m - mh.astype(F32)).astype(BF)

    event(13, None)
    gain(13, 0)
    c_psel = remote(psel, prem, pair_s.at[2], pair_r.at[2], partner)
    c_psel.start()
    lax.fori_loop(0, 8, turn_own, 0)

    inv_root = 1.0 / math.sqrt(8192.0)

    scale = 0.5 * inv_root

    place = {1: 1, 3: 2, 2: 3}

    def send_s(k):
        return remote(sall.at[0], sall.at[place[k]], s_s.at[k - 1], s_r.at[k - 1], first(k))

    c_psel.wait_recv()
    bmap = ((psel[0] + prem[0]) * inv_root).astype(BF)
    cmap = ((psel[1] + prem[1]) * inv_root).astype(BF)
    d_in = dot(mt2[0], cmap) + dot(mt2[1], cmap)
    d_out = dot(m2[0], bmap) + dot(m2[1], bmap)
    sall[0] = jnp.concatenate([d_in, d_out], axis=1).astype(BF)
    for k in (2, 1, 3):
        send_s(k).start()
    c_sg = pltpu.make_async_copy(sall.at[0, mine], sg_hbm, outs.at[0])
    c_sg.start()
    sel[:, 0:T] = bmap
    sel[:, T : 2 * T] = cmap

    inter = dot(sel[mine, 0:T], sel[mine, T : 2 * T], 1, 1).astype(BF)
    across = (dot(sel[0:T, 0:T], sel[T : 2 * T, T : 2 * T], 1, 1) * (1 - s).astype(F32)).astype(BF)

    def grads(start, stop):
        def one(j, carry):
            for u in range(4):
                pair = 4 * j + u
                off = pl.ds(pl.multiple_of(pair * 128, 128), 128)
                dp = dy[:, off]
                lhs = jnp.concatenate([e_all[2 * pair] * inter, e_all[2 * pair + 1] * inter], axis=1)
                rhs = jnp.concatenate([jnp.where(low, dp, none), jnp.where(low, none, dp)], axis=0)
                out = dot(lhs, rhs) + ewx[:, off].astype(F32) * dot(across, gw[:, off])
                ig[:, off] = out.astype(BF)
            return carry

        lax.fori_loop(start // 4, stop // 4, one, 0)

    def ig_out(c):
        part = pl.ds(c * 2048, 2048)
        return pltpu.make_async_copy(ig.at[:, part], ig_hbm.at[:, part], outs.at[1 + c])

    def blocks(half):
        return pl.ds(pl.multiple_of(half * 4, 4), 4), pl.ds(pl.multiple_of(half * 512, 512), 512)

    def own_weight(half, carry):
        four, rows_of = blocks(half)
        gf[four] = dot(xt[rows_of, 0:256], sall[0]).reshape(4, 128, 256)
        return carry

    lax.fori_loop(0, 2, own_weight, 0)
    for k in range(1, 4):
        all_xr(k).wait_recv()

        def turn(zb, carry, k=k):
            at = place[k] * 256
            xt[pl.ds(pl.multiple_of(zb * 128, 128), 128), at : at + 256] = xr[k - 1, zb].T
            return carry

        lax.fori_loop(0, 8, turn, 0)
        send_dr(k).wait_recv()
    drift = dr[pl.ds(pl.multiple_of(p1 * 128, 128), 128), :]
    for k in range(3):
        drift = drift + dr16[k].astype(F32)
    gf[z] = gf[z] - drift * (1.0 / scale)
    grads(0, 16)
    ig_out(0).start()

    def send_p(k):
        return remote(gs.at[(p2 + k) % 4], r2.at[k - 1], p_s.at[k - 1], p_r.at[k - 1], second(k))

    send_s(1).wait_recv()
    send_s(3).wait_recv()

    def near_weight(half, carry):
        four, rows_of = blocks(half)
        gf[four] += dot(xt[rows_of, 256:768], sall[1:3].reshape(512, 256)).reshape(4, 128, 256)
        return carry

    lax.fori_loop(0, 2, near_weight, 0)
    send_s(2).wait_recv()

    def far_weight(half, carry):
        four, rows_of = blocks(half)
        g = (gf[four] + dot(xt[rows_of, 768:1024], sall[3]).reshape(4, 128, 256)) * scale
        gf[four] = g
        for q in range(4):
            gs[q, four] = g[:, q * 32 : (q + 1) * 32].astype(BF)
        return carry

    lax.fori_loop(0, 2, far_weight, 0)
    for k in (2, 1, 3):
        send_p(k).start()
    grads(16, 32)
    ig_out(1).start()

    def send_z(k):
        return remote(t2b.at[(z + k) % 8], r3.at[k - 1], z_s.at[k - 1], z_r.at[k - 1], along(k))

    total = gf[:, pl.ds(pl.multiple_of(p2 * 32, 32), 32), :]
    for k in (1, 3, 2):
        send_p(k).wait_recv()
        total = total + r2[k - 1].astype(F32)
    t2[...] = total
    t2b[...] = total.astype(BF)
    for k in (4, 3, 5, 2, 6, 1, 7):
        send_z(k).start()
    grads(32, 48)
    ig_out(2).start()
    mine_at = p1 * 4 + p2

    def plane(k):
        at = dl.at[mine_at]
        device = {"seq": s, "dp": z, "island": (y + k // 4) % 4 * 4 + (x + k % 4) % 4}
        return remote(at, at, a_s.at[k - 1], a_r.at[k - 1], device)

    part = t2[z]
    for k in range(1, 8):
        send_z(k).wait_recv()
        part = part + r3[k - 1].astype(F32)
    dl[mine_at] = (part * (1.0 / 16.0)).astype(BF)

    for k in sorted(range(1, 16), key=lambda k: -(min(k // 4, 4 - k // 4) + min(k % 4, 4 - k % 4))):
        plane(k).start()
    grads(48, 64)
    ig_out(3).start()

    def drain(j, carry):
        right(j, z, 0).wait_send()
        left(j, z, 0).wait_send()
        return carry

    lax.fori_loop(0, EVENTS, drain, 0)
    c_xs.wait_send()
    c_psel.wait_send()

    @pl.when(s == 0)
    def _():
        c_mb0.wait_send()

    @pl.when(s == 1)
    def _():
        c_gw.wait_send()
        c_mb1.wait_send()

    for k in range(1, 4):
        all_xr(k).wait_send()
        send_dr(k).wait_send()
        send_s(k).wait_send()
        send_p(k).wait_send()
    for k in range(1, 8):
        send_z(k).wait_send()

    def arrived(k, carry):
        oy = (y + 4 - k // 4) % 4
        ox = (x + 4 - k % 4) % 4
        at = dl.at[(ox + s * (oy - ox)) * 4 + oy + s * (ox - oy)]
        remote(at, at, a_s.at[k - 1], a_r.at[k - 1], partner).wait_recv()
        return carry

    lax.fori_loop(1, 16, arrived, 0)
    c_delta = pltpu.make_async_copy(dl, delta_hbm, outs.at[5])
    c_delta.start()

    def left_here(k, carry):
        plane(k).wait_send()
        return carry

    lax.fori_loop(1, 16, left_here, 0)
    c_sg.wait()
    for c in range(4):
        ig_out(c).wait()
    c_delta.wait()


def finish(ig, sg, dl, mo, ow, ig_out, sg_out, mo_out, ow_out, igv, sgv, dlv, mov, owv, nmv, nov, ins, outs):
    loads = [
        pltpu.make_async_copy(dl, dlv, ins.at[0]),
        pltpu.make_async_copy(mo, mov, ins.at[1]),
        pltpu.make_async_copy(ow, owv, ins.at[2]),
        pltpu.make_async_copy(sg, sgv, ins.at[3]),
    ]
    parts = [pl.ds(32 * c, 32) for c in range(4)]
    moves = [pltpu.make_async_copy(ig.at[p], igv.at[p], ins.at[4 + c]) for c, p in enumerate(parts)]
    for c in loads + moves:
        c.start()
    ends = []
    for c, p in enumerate(parts):
        moves[c].wait()
        ends.append(pltpu.make_async_copy(igv.at[p], ig_out.at[p], outs.at[4 + c]))
        ends[c].start()
    for c in loads:
        c.wait()
    c_sg = pltpu.make_async_copy(sgv, sg_out, outs.at[1])
    c_sg.start()
    delta = dlv[...].reshape(512, 256).astype(F32)
    momentum = 0.9 * mov[...] + delta
    nmv[...] = momentum
    c_mo = pltpu.make_async_copy(nmv, mo_out, outs.at[2])
    c_mo.start()
    nov[...] = owv[...] - 0.7 * (delta + 0.9 * momentum)
    c_ow = pltpu.make_async_copy(nov, ow_out, outs.at[3])
    c_ow.start()
    for c in ends + [c_sg, c_mo, c_ow]:
        c.wait()


def local(layer_input, inner_acts, out_grad, step_sizes, outer_weight, island_drift, momentum):
    anyspec = pl.BlockSpec(memory_space=pl.ANY)
    dma = pltpu.SemaphoreType.DMA
    vm = pltpu.VMEM
    in_grad, sel_grad, delta = pl.pallas_call(
        kernel,
        out_shape=(
            jax.ShapeDtypeStruct((T, 8192), BF),
            jax.ShapeDtypeStruct((T, 256), BF),
            jax.ShapeDtypeStruct((16, 32, 256), BF),
        ),
        in_specs=[pl.BlockSpec(memory_space=pltpu.HBM)] * 6,
        out_specs=(anyspec, anyspec, anyspec),
        scratch_shapes=[
            vm((512, 256), F32),
            vm((512, 256), F32),
            vm((T, HEADS), F32),
            vm((T, 8192), BF),
            vm((T, 8192), BF),
            vm((8, 4, 128, 256), BF),
            vm((256, 4096), BF),
            vm((3, 8, 256, 128), BF),
            vm((1024, 1024), BF),
            vm((4, 128, 256), BF),
            vm((3, 128, 256), BF),
            vm((T, HEADS), F32),
            vm((HEADS, T), F32),
            vm((T, T), F32),
            vm((T, 2 * T), BF),
            vm((T, 8192), BF),
            vm((T, 8192), BF),
            vm((T, 8192), BF),
            vm((HEADS, T, T), BF),
            vm((T, 8192), BF),
            vm((3, T, T), F32),
            vm((2, 256, 256), BF),
            vm((2, 256, 256), BF),
            vm((2, 256, T), F32),
            vm((2, 256, T), F32),
            vm((256, 256), BF),
            vm((4, 256, 256), BF),
            vm((8, 128, 256), F32),
            vm((4, 8, 32, 256), BF),
            vm((3, 8, 32, 256), BF),
            vm((8, 32, 256), F32),
            vm((8, 32, 256), BF),
            vm((7, 32, 256), BF),
            vm((16, 32, 256), BF),
            dma((6,)),
            dma((2, EVENTS)),
            dma((2, EVENTS)),
            dma((5,)),
            dma((5,)),
            dma((3,)), dma((3,)),
            dma((3,)), dma((3,)),
            dma((3,)), dma((3,)),
            dma((3,)), dma((3,)),
            dma((7,)), dma((7,)),
            dma((15,)), dma((15,)),
            dma((6,)),
        ],
        compiler_params=pltpu.CompilerParams(
            collective_id=0, has_side_effects=True, vmem_limit_bytes=VMEM_LIMIT
        ),
    )(
        layer_input[0, 0], inner_acts[0, 0], out_grad[0, 0], step_sizes[0, 0], outer_weight, island_drift[0]
    )
    in_grad, sel_grad, new_momentum, new_outer = pl.pallas_call(
        finish,
        out_shape=(
            jax.ShapeDtypeStruct((T, 8192), BF),
            jax.ShapeDtypeStruct((T, 256), BF),
            jax.ShapeDtypeStruct((512, 256), F32),
            jax.ShapeDtypeStruct((512, 256), F32),
        ),
        in_specs=[anyspec] * 5,
        out_specs=(pl.BlockSpec(memory_space=pltpu.HBM),) * 4,
        scratch_shapes=[
            vm((T, 8192), BF), vm((T, 256), BF), vm((16, 32, 256), BF),
            vm((512, 256), F32), vm((512, 256), F32), vm((512, 256), F32), vm((512, 256), F32),
            dma((8,)), dma((8,)),
        ],
        compiler_params=pltpu.CompilerParams(vmem_limit_bytes=FINISH_LIMIT),
    )(in_grad, sel_grad, delta, momentum, outer_weight)
    return (in_grad[None, None], sel_grad[None, None], new_momentum, new_outer)


def solution(mesh):
    acts = P("island", "dp", "seq", None)
    rows = P(("seq", "dp"), None)
    return jax.shard_map(
        local,
        mesh=mesh,
        in_specs=(acts, acts, acts, acts, rows, P("island", ("seq", "dp"), None), rows),
        out_specs=(acts, acts, rows, rows),
        check_vma=False,
    )
```
